32 devices in a mesh: dp: 8 (over z, x), tensor: 4 (over y, core).
Axes of the slice: x: 2, y: 2, z: 4, core: 2. Of those that a mesh axis runs over, the one named last changes fastest.
Arguments:
- hidden: bfloat16 [1024, 28672], P('dp', 'tensor'), may hold values from -6 to 6
- out_grad: bfloat16 [1024, 8192], P('dp'), may hold values from -6 to 6
- prev_hidden: bfloat16 [1024, 28672], P('dp', 'tensor'), may hold values from -6 to 6
- prev_grad: bfloat16 [1024, 8192], P('dp'), may hold values from -6 to 6
- prev_basis: float32 [28672, 32], P('tensor'), may hold values from -6 to 6
- warm_start: float32 [8192, 32], replicated, may hold values from -0.17 to 0.17
Outputs:
- new_basis: float32 [28672, 32], P('tensor')
- new_factor: float32 [8192, 32], P('dp')
The draws below stay inside these ranges and needn't reach their ends.
All inputs are finite; a program needn't handle non-finite values.
Results may differ from the reference program's by a relative error of at most 0.007.
Values sent between devices are 32-bit elements; how exact they have to be, the bound alone decides.
No kernel may reach another device: no remote copies, remote signals or barrier semaphores. Data moves between devices by JAX's collectives and lax.ppermute only.
A program may use at most 64 MiB of HBM per device.

```python
import jax
import jax.numpy as jnp
from jax import lax

D = 8192
FF = 28672
R = 32
TOKENS = 1024
N_DP = 8


def strengthened(array, rng, source, target, parts, factor):
    def block_of(dim):
        return (jnp.arange(array.shape[dim]) // (array.shape[dim] // parts)).reshape((-1,) + (1,) * (array.ndim - 1 - dim))

    near = jax.random.permutation(rng, parts)[block_of(target)]
    far = (block_of(target) + parts // 2) % parts
    return jnp.where((block_of(source) == near) | (block_of(source) == far), factor * array, array)


def levels(own_key, extent, shards, smallest, largest):
    factor_of = 1.0
    for dim, shards_of in shards:
        draws = jax.random.uniform(jax.random.fold_in(jax.random.fold_in(own_key, 6), dim), (shards_of,), jnp.float32, smallest / len(shards), largest / len(shards))
        factor_of = factor_of * jnp.repeat(jnp.exp(draws), extent[dim] // shards_of).reshape((-1,) + (1,) * (len(extent) - 1 - dim))
    return factor_of


def bell_draw(key, extent, width, reach, shards=(), held_as=jnp.bfloat16):
    array = width * jax.random.normal(key, extent, jnp.float32)
    if shards:
        array = array * levels(key, extent, shards, -0.22, 0.18)
    return jnp.clip(array, -reach, reach).astype(held_as)


def bell_draw_with(key, shape, scale, limit, split, heavy, held_as=jnp.bfloat16):
    array = scale * jax.random.normal(key, shape, jnp.float32)
    if split:
        array = array * levels(key, shape, split, -0.22, 0.18)
    return jnp.clip(strengthened(array, jax.random.fold_in(key, 3), *heavy), -limit, limit).astype(held_as)


def setup_inputs(seed: int = 0) -> dict:
    keys = jax.random.split(jax.random.key(seed), 7)
    return {
        "hidden": bell_draw(keys[0], (TOKENS, FF), 1.0, 6.0, ((0, 8), (1, 4))),
        "out_grad": bell_draw_with(keys[1], (TOKENS, D), 1.0, 6.0, ((0, 8),), (0, 1, 8, 2.0)),
        "prev_hidden": bell_draw(keys[2], (TOKENS, FF), 1.0, 6.0, ((0, 8), (1, 4))),
        "prev_grad": bell_draw_with(keys[3], (TOKENS, D), 1.0, 6.0, ((0, 8),), (0, 1, 8, 2.0)),
        "prev_basis": bell_draw(keys[4], (FF, R), 1.0, 6.0, ((0, 4),), jnp.float32),
        "warm_start": bell_draw(keys[5], (D, R), 0.028, 0.17, (), jnp.float32),
    }


def reference(hidden, out_grad, prev_hidden, prev_grad, prev_basis, warm_start):
    highest = lax.Precision.HIGHEST
    warm_low = warm_start.astype(jnp.bfloat16)
    projected = jnp.dot(out_grad.astype(jnp.float32), warm_low.astype(jnp.float32), preferred_element_type=jnp.float32).astype(jnp.bfloat16)
    projected_prev = jnp.dot(prev_grad.astype(jnp.float32), warm_low.astype(jnp.float32), preferred_element_type=jnp.float32).astype(jnp.bfloat16)
    coupling = jnp.dot(warm_start.T, warm_start, precision=highest)
    summed = jnp.dot(hidden.T.astype(jnp.float32), projected.astype(jnp.float32), preferred_element_type=jnp.float32) + jnp.dot(prev_hidden.T.astype(jnp.float32), projected_prev.astype(jnp.float32), preferred_element_type=jnp.float32)
    p_mean = summed / N_DP - jnp.dot(prev_basis, coupling, precision=highest)
    gram_matrix = jnp.dot(p_mean.T, p_mean, precision=highest)
    lower = jnp.linalg.cholesky(gram_matrix)
    norm_scale = jnp.sqrt(jnp.float32(FF))
    new_basis = norm_scale * jax.scipy.linalg.solve_triangular(lower, p_mean.T, lower=True).T
    basis_low = new_basis.astype(jnp.bfloat16)
    pulled = jnp.dot(hidden.astype(jnp.float32), basis_low.astype(jnp.float32), preferred_element_type=jnp.float32).astype(jnp.bfloat16)
    pulled_prev = jnp.dot(prev_hidden.astype(jnp.float32), basis_low.astype(jnp.float32), preferred_element_type=jnp.float32).astype(jnp.bfloat16)
    cross_basis = jnp.dot(prev_basis.T, new_basis, precision=highest)
    summed_q = jnp.dot(out_grad.T.astype(jnp.float32), pulled.astype(jnp.float32), preferred_element_type=jnp.float32) + jnp.dot(prev_grad.T.astype(jnp.float32), pulled_prev.astype(jnp.float32), preferred_element_type=jnp.float32)
    new_factor = (summed_q / N_DP - jnp.dot(warm_start, cross_basis, precision=highest)) / norm_scale
    return (new_basis, new_factor)
```

```python
import functools

import jax
import jax.numpy as jnp
from jax import lax
from jax.experimental import pallas as pl
from jax.experimental.pallas import tpu as pltpu
from jax.sharding import PartitionSpec as P

F32 = jnp.float32
BF16 = jnp.bfloat16
SQUARE = 4
NT = (((1,), (1,)), ((), ()))
NN = (((1,), (0,)), ((), ()))
VMEM_SPEC = pl.BlockSpec(memory_space=pltpu.VMEM)
ANY_SPEC = pl.BlockSpec(memory_space=pl.ANY)


def orthonormal(rows_in, gram_matrix, norm_scale):
    lower = jnp.linalg.cholesky(gram_matrix)
    return norm_scale * jax.scipy.linalg.solve_triangular(lower, rows_in.T, lower=True).T


def plain_on_device(hidden, out_grad, prev_hidden, prev_grad, prev_basis, warm_start, *, norm_scale):
    highest = lax.Precision.HIGHEST
    replicas = lax.axis_size("dp")
    warm_low = warm_start.astype(BF16)
    projected = jnp.dot(out_grad, warm_low, preferred_element_type=F32).astype(BF16)
    projected_prev = jnp.dot(prev_grad, warm_low, preferred_element_type=F32).astype(BF16)
    coupling = jnp.dot(warm_start.T, warm_start, precision=highest)
    summed = jnp.einsum("tf,tr->fr", hidden, projected, preferred_element_type=F32)
    summed = summed + jnp.einsum(
        "tf,tr->fr", prev_hidden, projected_prev, preferred_element_type=F32
    )
    local_p = (summed - jnp.dot(prev_basis, coupling, precision=highest)) / replicas
    p_mean = lax.psum(local_p, "dp")
    gram_matrix = lax.psum(jnp.dot(p_mean.T, p_mean, precision=highest), "tensor")
    new_basis = orthonormal(p_mean, gram_matrix, norm_scale)
    basis_low = new_basis.astype(BF16)
    pulled = jnp.dot(hidden, basis_low, preferred_element_type=F32).astype(BF16)
    pulled_prev = jnp.dot(prev_hidden, basis_low, preferred_element_type=F32).astype(BF16)
    cross_basis = jnp.dot(prev_basis.T, new_basis, precision=highest)
    summed_q = jnp.einsum("td,tr->dr", out_grad, pulled, preferred_element_type=F32)
    summed_q = summed_q + jnp.einsum(
        "td,tr->dr", prev_grad, pulled_prev, preferred_element_type=F32
    )
    local_q = (summed_q - jnp.dot(warm_start, cross_basis, precision=highest)) / replicas
    row_count = warm_start.shape[0] // replicas
    summed_all = lax.psum(local_q, ("dp", "tensor"))
    owned_rows = lax.dynamic_slice_in_dim(
        summed_all, lax.axis_index("dp") * row_count, row_count, 0
    )
    return (new_basis, owned_rows / norm_scale)


def split(x, terms):
    parts = []
    for i in range(terms):
        part = x.astype(BF16)
        parts.append(part)
        if i + 1 < terms:
            x = x - part.astype(F32)
    return parts


def dot(a, b, dims, precision=None):
    return lax.dot_general(a, b, dims, preferred_element_type=F32, precision=precision)


def chunks(extent, count):
    step = extent // count
    return [pl.ds(i * step, step) for i in range(count)]


def left_factor_kernel(w_ref, o_ref, o2_ref, h_ref, h2_ref, *refs):
    pieces, (wv, ov, hv, sem) = refs[:SQUARE], refs[SQUARE:]
    q = lax.axis_index("dp") % SQUARE
    rows = wv.shape[0] // SQUARE
    tokens = o_ref.shape[0]
    o_cuts, h_cuts = chunks(o_ref.shape[1], 4), chunks(h_ref.shape[1], 4)
    copies = []
    for m in range(SQUARE):
        copies.append(
            pltpu.make_async_copy(
                w_ref.at[pl.ds((q ^ m) * rows, rows), :], wv.at[pl.ds(m * rows, rows), :], sem.at[m]
            )
        )
    for i, cut in enumerate(o_cuts):
        for j, ref in enumerate((o_ref, o2_ref)):
            copies.append(
                pltpu.make_async_copy(
                    ref.at[:, cut], ov.at[pl.ds(j * tokens, tokens), cut], sem.at[4 + 2 * i + j]
                )
            )
    for i, cut in enumerate(h_cuts):
        for j, ref in enumerate((h_ref, h2_ref)):
            copies.append(
                pltpu.make_async_copy(
                    ref.at[:, cut], hv.at[pl.ds(j * tokens, tokens), cut], sem.at[12 + 2 * i + j]
                )
            )
    for copy in copies:
        copy.start()
    for copy in copies[:4]:
        copy.wait()
    projected = jnp.zeros((wv.shape[0], 2 * tokens), F32)
    for i, cut in enumerate(o_cuts):
        copies[4 + 2 * i].wait()
        copies[5 + 2 * i].wait()
        projected += dot(wv[:, cut].astype(BF16), ov[:, cut], NT)
    projected = projected.astype(BF16)
    for i, cut in enumerate(h_cuts):
        copies[12 + 2 * i].wait()
        copies[13 + 2 * i].wait()
        summed = dot(projected, hv[:, cut], NN)
        for m in range(SQUARE):
            pieces[m][:, cut] = summed[m * rows : (m + 1) * rows]


def feedback_kernel(w_ref, b_ref, out_ref, c_ref):
    q = lax.axis_index("dp") % SQUARE
    rows = out_ref.shape[0]
    rank = w_ref.shape[0]
    total = jnp.zeros((3 * rank, 3 * rank), F32)
    for cut in chunks(w_ref.shape[1], 4):
        stacked = jnp.concatenate(split(w_ref[:, cut], 3), axis=0)
        total += dot(stacked, stacked, NT)
    total = total[:rank] + total[rank : 2 * rank] + total[2 * rank :]
    c_ref[...] = total[:, :rank] + total[:, rank : 2 * rank] + total[:, 2 * rank :]
    own = c_ref[pl.ds(q * rows, rows), :]
    for cut in chunks(b_ref.shape[1], 4):
        out_ref[:, cut] = dot(own, b_ref[:, cut], NN, lax.Precision.HIGHEST)


def pull_kernel(s0, s1, s2, s3, h_ref, h2_ref, keep_ref, send_ref, v_ref):
    q = lax.axis_index("dp") % SQUARE
    core = lax.axis_index("tensor") % 2
    tokens = h_ref.shape[0]
    rows, half = s0.shape[0], keep_ref.shape[0]
    rank = SQUARE * rows
    now = jnp.zeros((2 * rank, tokens), F32)
    prev = jnp.zeros((2 * rank, tokens), F32)
    for cut in chunks(h_ref.shape[1], 4):
        p = jnp.concatenate([s[:, cut] for s in (s0, s1, s2, s3)], axis=0)
        stacked = jnp.concatenate(split(p, 2), axis=0)
        now += dot(stacked, h_ref[:, cut], NT)
        prev += dot(stacked, h2_ref[:, cut], NT)
    now = now[:rank] + now[rank:]
    prev = prev[:rank] + prev[rank:]
    for m in range(SQUARE):
        place = pl.ds((q ^ m) * rows, rows)
        v_ref[place, :tokens] = now[m * rows : (m + 1) * rows]
        v_ref[place, tokens:] = prev[m * rows : (m + 1) * rows]
    keep_ref[...] = v_ref[pl.ds(core * half, half), :]
    send_ref[...] = v_ref[pl.ds((1 - core) * half, half), :]


def push_kernel(keep_ref, got_ref, o_ref, o2_ref, *outs):
    me = lax.axis_index("dp")
    tokens = o_ref.shape[0]
    half, width = outs[0].shape[1:]
    v = jnp.concatenate(split(keep_ref[...] + got_ref[...], 2), axis=0)
    for m in range(SQUARE):
        for z in range(2):
            cut = pl.ds(pl.multiple_of((me ^ m ^ (SQUARE * z)) * width, width), width)
            both = dot(v[:, :tokens], o_ref[:, cut], NN) + dot(v[:, tokens:], o2_ref[:, cut], NN)
            outs[m][z] = both[:half] + both[half:]


def gram_kernel(s0, s1, s2, s3, b_ref, out_ref, p_ref):
    q = lax.axis_index("dp") % SQUARE
    rows = s0.shape[0]
    rank = SQUARE * rows
    for m, s in enumerate((s0, s1, s2, s3)):
        p_ref[pl.ds((q ^ m) * rows, rows), :] = s[...]
    total = jnp.zeros((3 * rank, 6 * rank), F32)
    for cut in chunks(b_ref.shape[1], 4):
        p = split(p_ref[:, cut], 3)
        b = split(b_ref[:, cut], 3)
        total += dot(jnp.concatenate(p, axis=0), jnp.concatenate(p + b, axis=0), NT)
    total = total[:rank] + total[rank : 2 * rank] + total[2 * rank :]
    gram = total[:, :rank] + total[:, rank : 2 * rank] + total[:, 2 * rank : 3 * rank]
    cross = total[:, 3 * rank : 4 * rank] + total[:, 4 * rank : 5 * rank] + total[:, 5 * rank :]
    out_ref[...] = jnp.zeros_like(out_ref)
    out_ref[:, :rank] = gram
    out_ref[:, rank : 2 * rank] = cross


def cholesky_kernel(in_ref, out_ref):
    rank = in_ref.shape[0]
    shape = in_ref.shape
    row = lax.broadcasted_iota(jnp.int32, shape, 0)
    lane = lax.broadcasted_iota(jnp.int32, shape, 1)
    a = jnp.where(lane == row + 2 * rank, 1.0, in_ref[...])
    for k in range(rank):
        pivot = a[k : k + 1, k : k + 1]
        scale = 1.0 / jnp.sqrt(pivot)
        top = a[k : k + 1, :] * scale
        below = jnp.where(row[:, :1] > k, a[:, k : k + 1] * scale, 0.0)
        a = jnp.where(row == k, top, a - below * top)
    out_ref[...] = a


def basis_kernel(s0, s1, s2, s3, l_ref, out_ref, p_ref, *, norm_scale):
    q = lax.axis_index("dp") % SQUARE
    rows = s0.shape[0]
    rank = SQUARE * rows
    inverse = l_ref[:, 2 * rank : 3 * rank] * norm_scale
    for m, s in enumerate((s0, s1, s2, s3)):
        p_ref[pl.ds((q ^ m) * rows, rows), :] = s[...]
    for cut in chunks(out_ref.shape[1], 4):
        out_ref[:, cut] = dot(inverse, p_ref[:, cut], NN, lax.Precision.HIGHEST)


def factor_kernel(t_ref, u_ref, l_ref, w_ref, out_ref, z_ref, wv, sem, *, replicas):
    core = lax.axis_index("tensor") % 2
    half, width = t_ref.shape
    rank = 2 * half
    start = pl.multiple_of(lax.axis_index("dp") * width, width)
    copy = pltpu.make_async_copy(w_ref.at[:, pl.ds(start, width)], wv, sem)
    copy.start()
    z_ref[pl.ds(core * half, half), :] = t_ref[...] * (1.0 / replicas)
    z_ref[pl.ds((1 - core) * half, half), :] = u_ref[...] * (1.0 / replicas)
    highest = lax.Precision.HIGHEST
    out = dot(l_ref[:, 2 * rank : 3 * rank], z_ref[...], NN, highest)
    copy.wait()
    out_ref[...] = out - dot(l_ref[:, rank : 2 * rank], wv[...], NN, highest)


def call(kernel, outs, specs, scratch=(), flops=0, moved=0):
    return pl.pallas_call(
        kernel,
        out_shape=[jax.ShapeDtypeStruct(shape, F32) for shape in outs],
        in_specs=specs,
        out_specs=[VMEM_SPEC] * len(outs),
        scratch_shapes=scratch,
        compiler_params=pltpu.CompilerParams(vmem_limit_bytes=32 << 20),
        cost_estimate=pl.CostEstimate(flops=flops, bytes_accessed=moved, transcendentals=0),
    )


def swap_dp(x, m):
    n = lax.axis_size("dp")
    return lax.ppermute(x, "dp", [(i, i ^ m) for i in range(n)])


def swap_tensor(x, m):
    n = lax.axis_size("tensor")
    return lax.ppermute(x, "tensor", [(i, i ^ m) for i in range(n)])


def swap_both(x, md, mt):
    n, k = lax.axis_size("dp"), lax.axis_size("tensor")
    pairs = [(i * k + t, (i ^ md) * k + (t ^ mt)) for i in range(n) for t in range(k)]
    return lax.ppermute(x, ("dp", "tensor"), pairs)


def on_device(hidden, out_grad, prev_hidden, prev_grad, prev_basis, warm_start, *, norm_scale):
    replicas = lax.axis_size("dp")
    tokens, units = hidden.shape
    width = out_grad.shape[1]
    rank = warm_start.shape[1]
    rows, half, owned = rank // SQUARE, rank // 2, width // replicas
    w, b = warm_start.T, prev_basis.T
    piece = (rows, units)

    terms = call(
        left_factor_kernel,
        [piece] * SQUARE,
        [ANY_SPEC] * 5,
        [
            pltpu.VMEM((rank, width), F32),
            pltpu.VMEM((2 * tokens, width), BF16),
            pltpu.VMEM((2 * tokens, units), BF16),
            pltpu.SemaphoreType.DMA((20,)),
        ],
        flops=4 * tokens * rank * (units + width),
        moved=4 * tokens * (units + width) + 4 * rank * (units + width),
    )(w, out_grad, prev_grad, hidden, prev_hidden)
    got = [swap_dp(terms[m], m) for m in range(1, SQUARE)]
    (feedback,) = call(
        feedback_kernel,
        [piece],
        [VMEM_SPEC] * 2,
        [pltpu.VMEM((rank, rank), F32)],
        flops=2 * rank * rank * (units + width),
        moved=4 * rank * (units + width),
    )(w, b)
    summed = terms[0] + got[0] + got[1] + got[2]
    own = (summed + swap_dp(summed, SQUARE)) * (1.0 / replicas) - feedback
    p = [own] + [swap_dp(own, m) for m in range(1, SQUARE)]

    keep, send = call(
        pull_kernel,
        [(half, 2 * tokens)] * 2,
        [VMEM_SPEC] * 6,
        [pltpu.VMEM((rank, 2 * tokens), F32)],
        flops=8 * tokens * rank * units,
        moved=4 * tokens * units + 4 * rank * units,
    )(*p, hidden, prev_hidden)
    other = swap_tensor(send, 1)
    (gram,) = call(
        gram_kernel,
        [(rank, 128)],
        [VMEM_SPEC] * 5,
        [pltpu.VMEM((rank, units), F32)],
        flops=4 * rank * rank * units,
        moved=8 * rank * units,
    )(*p, b)
    parts = call(
        push_kernel,
        [(2, half, owned)] * SQUARE,
        [VMEM_SPEC] * 4,
        flops=8 * tokens * half * width,
        moved=4 * tokens * width + 4 * half * width,
    )(keep, other, out_grad, prev_grad)
    came = [swap_dp(parts[m], m) for m in range(1, SQUARE)]

    gram = gram + swap_tensor(gram, 1)
    gram = gram + swap_tensor(gram, 2)
    (solved,) = call(
        cholesky_kernel, [(rank, 128)], [VMEM_SPEC], flops=rank**3, moved=8 * rank * 128
    )(gram)
    (basis,) = call(
        functools.partial(basis_kernel, norm_scale=norm_scale),
        [(rank, units)],
        [VMEM_SPEC] * 5,
        [pltpu.VMEM((rank, units), F32)],
        flops=2 * rank * rank * units,
        moved=8 * rank * units,
    )(*p, solved)

    near = parts[0][0] + came[0][0] + came[1][0] + came[2][0]
    far = parts[0][1] + came[0][1] + came[1][1] + came[2][1]
    mine = near + swap_both(far, SQUARE, 0) + swap_both(near, 0, 2) + swap_both(far, SQUARE, 2)
    (factor,) = call(
        functools.partial(factor_kernel, replicas=replicas),
        [(rank, owned)],
        [VMEM_SPEC] * 3 + [ANY_SPEC],
        [pltpu.VMEM((rank, owned), F32), pltpu.VMEM((rank, owned), F32), pltpu.SemaphoreType.DMA],
        flops=4 * rank * rank * owned,
        moved=12 * rank * owned,
    )(mine, swap_tensor(mine, 1), solved, w)
    return (basis.T, factor.T)


def fits(mesh, dp=8, tensor=4):
    return mesh.shape["dp"] == dp and mesh.shape["tensor"] == tensor


def solution(mesh):
    def whole(hidden, out_grad, prev_hidden, prev_grad, prev_basis, warm_start):
        norm_scale = float(prev_basis.shape[0]) ** 0.5
        body = on_device if fits(mesh) else plain_on_device
        return jax.shard_map(
            functools.partial(body, norm_scale=norm_scale),
            mesh=mesh,
            in_specs=(
                P("dp", "tensor"),
                P("dp", None),
                P("dp", "tensor"),
                P("dp", None),
                P("tensor", None),
                P(),
            ),
            out_specs=(P("tensor", None), P("dp", None)),
            check_vma=False,
        )(hidden, out_grad, prev_hidden, prev_grad, prev_basis, warm_start)

    return whole
```

```python
import functools

import jax
import jax.numpy as jnp
from jax import lax
from jax.experimental import pallas as pl
from jax.experimental.pallas import tpu as pltpu
from jax.sharding import PartitionSpec as P

F32 = jnp.float32
BF16 = jnp.bfloat16
SQUARE = 4
NT = (((1,), (1,)), ((), ()))
NN = (((1,), (0,)), ((), ()))
VMEM_SPEC = pl.BlockSpec(memory_space=pltpu.VMEM)
ANY_SPEC = pl.BlockSpec(memory_space=pl.ANY)
HBM_SPEC = pl.BlockSpec(memory_space=pltpu.HBM)


def orthonormal(rows_in, gram_matrix, norm_scale):
    lower = jnp.linalg.cholesky(gram_matrix)
    return norm_scale * jax.scipy.linalg.solve_triangular(lower, rows_in.T, lower=True).T


def plain_on_device(hidden, out_grad, prev_hidden, prev_grad, prev_basis, warm_start, *, norm_scale):
    highest = lax.Precision.HIGHEST
    replicas = lax.axis_size("dp")
    warm_low = warm_start.astype(BF16)
    projected = jnp.dot(out_grad, warm_low, preferred_element_type=F32).astype(BF16)
    projected_prev = jnp.dot(prev_grad, warm_low, preferred_element_type=F32).astype(BF16)
    coupling = jnp.dot(warm_start.T, warm_start, precision=highest)
    summed = jnp.einsum("tf,tr->fr", hidden, projected, preferred_element_type=F32)
    summed = summed + jnp.einsum(
        "tf,tr->fr", prev_hidden, projected_prev, preferred_element_type=F32
    )
    local_p = (summed - jnp.dot(prev_basis, coupling, precision=highest)) / replicas
    p_mean = lax.psum(local_p, "dp")
    gram_matrix = lax.psum(jnp.dot(p_mean.T, p_mean, precision=highest), "tensor")
    new_basis = orthonormal(p_mean, gram_matrix, norm_scale)
    basis_low = new_basis.astype(BF16)
    pulled = jnp.dot(hidden, basis_low, preferred_element_type=F32).astype(BF16)
    pulled_prev = jnp.dot(prev_hidden, basis_low, preferred_element_type=F32).astype(BF16)
    cross_basis = jnp.dot(prev_basis.T, new_basis, precision=highest)
    summed_q = jnp.einsum("td,tr->dr", out_grad, pulled, preferred_element_type=F32)
    summed_q = summed_q + jnp.einsum(
        "td,tr->dr", prev_grad, pulled_prev, preferred_element_type=F32
    )
    local_q = (summed_q - jnp.dot(warm_start, cross_basis, precision=highest)) / replicas
    row_count = warm_start.shape[0] // replicas
    summed_all = lax.psum(local_q, ("dp", "tensor"))
    owned_rows = lax.dynamic_slice_in_dim(
        summed_all, lax.axis_index("dp") * row_count, row_count, 0
    )
    return (new_basis, owned_rows / norm_scale)


def split(x, terms):
    parts = []
    for i in range(terms):
        part = x.astype(BF16)
        parts.append(part)
        if i + 1 < terms:
            x = x - part.astype(F32)
    return parts


def dot(a, b, dims, precision=None):
    return lax.dot_general(a, b, dims, preferred_element_type=F32, precision=precision)


def chunks(extent, count):
    step = extent // count
    return [pl.ds(i * step, step) for i in range(count)]


def left_factor_kernel(w_ref, o_ref, o2_ref, h_ref, h2_ref, *refs):
    pieces, (wv, ov, hv, sem) = refs[:SQUARE], refs[SQUARE:]
    q = lax.axis_index("dp") % SQUARE
    rows = wv.shape[0] // SQUARE
    tokens = o_ref.shape[0]
    o_cuts, h_cuts = chunks(o_ref.shape[1], 4), chunks(h_ref.shape[1], 4)
    copies = []
    for m in range(SQUARE):
        copies.append(
            pltpu.make_async_copy(
                w_ref.at[pl.ds((q ^ m) * rows, rows), :], wv.at[pl.ds(m * rows, rows), :], sem.at[m]
            )
        )
    for i, cut in enumerate(o_cuts):
        for j, ref in enumerate((o_ref, o2_ref)):
            copies.append(
                pltpu.make_async_copy(
                    ref.at[:, cut], ov.at[pl.ds(j * tokens, tokens), cut], sem.at[4 + 2 * i + j]
                )
            )
    for i, cut in enumerate(h_cuts):
        for j, ref in enumerate((h_ref, h2_ref)):
            copies.append(
                pltpu.make_async_copy(
                    ref.at[:, cut], hv.at[pl.ds(j * tokens, tokens), cut], sem.at[12 + 2 * i + j]
                )
            )
    for copy in copies:
        copy.start()
    for copy in copies[:4]:
        copy.wait()
    projected = jnp.zeros((wv.shape[0], 2 * tokens), F32)
    for i, cut in enumerate(o_cuts):
        copies[4 + 2 * i].wait()
        copies[5 + 2 * i].wait()
        projected += dot(wv[:, cut].astype(BF16), ov[:, cut], NT)
    projected = projected.astype(BF16)
    for i, cut in enumerate(h_cuts):
        copies[12 + 2 * i].wait()
        copies[13 + 2 * i].wait()
        summed = dot(projected, hv[:, cut], NN)
        for m in range(SQUARE):
            pieces[m][:, cut] = summed[m * rows : (m + 1) * rows]


def feedback_kernel(w_ref, b_ref, out_ref, c_ref):
    q = lax.axis_index("dp") % SQUARE
    rows = out_ref.shape[0]
    rank = w_ref.shape[0]
    total = jnp.zeros((3 * rank, 3 * rank), F32)
    for cut in chunks(w_ref.shape[1], 4):
        stacked = jnp.concatenate(split(w_ref[:, cut], 3), axis=0)
        total += dot(stacked, stacked, NT)
    total = total[:rank] + total[rank : 2 * rank] + total[2 * rank :]
    c_ref[...] = total[:, :rank] + total[:, rank : 2 * rank] + total[:, 2 * rank :]
    own = c_ref[pl.ds(q * rows, rows), :]
    for cut in chunks(b_ref.shape[1], 4):
        out_ref[:, cut] = dot(own, b_ref[:, cut], NN, lax.Precision.HIGHEST)


def pull_kernel(s0, s1, s2, s3, h_ref, h2_ref, keep_ref, send_ref, v_ref):
    q = lax.axis_index("dp") % SQUARE
    core = lax.axis_index("tensor") % 2
    tokens = h_ref.shape[0]
    rows, half = s0.shape[0], keep_ref.shape[0]
    rank = SQUARE * rows
    now = jnp.zeros((2 * rank, tokens), F32)
    prev = jnp.zeros((2 * rank, tokens), F32)
    for cut in chunks(h_ref.shape[1], 4):
        p = jnp.concatenate([s[:, cut] for s in (s0, s1, s2, s3)], axis=0)
        stacked = jnp.concatenate(split(p, 2), axis=0)
        now += dot(stacked, h_ref[:, cut], NT)
        prev += dot(stacked, h2_ref[:, cut], NT)
    now = now[:rank] + now[rank:]
    prev = prev[:rank] + prev[rank:]
    for m in range(SQUARE):
        place = pl.ds((q ^ m) * rows, rows)
        v_ref[place, :tokens] = now[m * rows : (m + 1) * rows]
        v_ref[place, tokens:] = prev[m * rows : (m + 1) * rows]
    keep_ref[...] = v_ref[pl.ds(core * half, half), :]
    send_ref[...] = v_ref[pl.ds((1 - core) * half, half), :]


def push_kernel(keep_ref, got_ref, o_ref, o2_ref, after_ref, *outs):
    me = lax.axis_index("dp")
    tokens = o_ref.shape[0]
    half, width = outs[0].shape[1:]
    v = jnp.concatenate(split(keep_ref[...] + got_ref[...], 2), axis=0)
    for m in range(SQUARE):
        for z in range(2):
            cut = pl.ds(pl.multiple_of((me ^ m ^ (SQUARE * z)) * width, width), width)
            both = dot(v[:, :tokens], o_ref[:, cut], NN) + dot(v[:, tokens:], o2_ref[:, cut], NN)
            outs[m][z] = both[:half] + both[half:]


def gram_kernel(s0, s1, s2, s3, b_ref, out_ref, p_ref):
    q = lax.axis_index("dp") % SQUARE
    rows = s0.shape[0]
    rank = SQUARE * rows
    for m, s in enumerate((s0, s1, s2, s3)):
        p_ref[pl.ds((q ^ m) * rows, rows), :] = s[...]
    total = jnp.zeros((3 * rank, 6 * rank), F32)
    for cut in chunks(b_ref.shape[1], 4):
        p = split(p_ref[:, cut], 3)
        b = split(b_ref[:, cut], 3)
        total += dot(jnp.concatenate(p, axis=0), jnp.concatenate(p + b, axis=0), NT)
    total = total[:rank] + total[rank : 2 * rank] + total[2 * rank :]
    gram = total[:, :rank] + total[:, rank : 2 * rank] + total[:, 2 * rank : 3 * rank]
    cross = total[:, 3 * rank : 4 * rank] + total[:, 4 * rank : 5 * rank] + total[:, 5 * rank :]
    out_ref[...] = jnp.zeros_like(out_ref)
    out_ref[:, :rank] = gram
    out_ref[:, rank : 2 * rank] = cross


def cholesky_kernel(in_ref, out_ref):
    rank = in_ref.shape[0]
    shape = in_ref.shape
    row = lax.broadcasted_iota(jnp.int32, shape, 0)
    lane = lax.broadcasted_iota(jnp.int32, shape, 1)
    a = jnp.where(lane == row + 2 * rank, 1.0, in_ref[...])
    for k in range(rank):
        pivot = a[k : k + 1, k : k + 1]
        scale = 1.0 / jnp.sqrt(pivot)
        top = a[k : k + 1, :] * scale
        below = jnp.where(row[:, :1] > k, a[:, k : k + 1] * scale, 0.0)
        a = jnp.where(row == k, top, a - below * top)
    out_ref[...] = a


def near_far_kernel(a_ref, b_ref, c_ref, d_ref, after_ref, near_ref, far_ref):
    near_ref[...] = a_ref[0] + b_ref[0] + c_ref[0] + d_ref[0]
    far_ref[...] = a_ref[1] + b_ref[1] + c_ref[1] + d_ref[1]


def total_kernel(a_ref, b_ref, c_ref, d_ref, after_ref, out_ref):
    out_ref[...] = a_ref[...] + b_ref[...] + c_ref[...] + d_ref[...]


def basis_kernel(s0, s1, s2, s3, l_ref, w_ref, out_ref, fix_ref, p_ref, *, norm_scale):
    q = lax.axis_index("dp") % SQUARE
    rows = s0.shape[0]
    rank = SQUARE * rows
    width = fix_ref.shape[1]
    highest = lax.Precision.HIGHEST
    inverse = l_ref[:, 2 * rank : 3 * rank] * norm_scale
    for m, s in enumerate((s0, s1, s2, s3)):
        p_ref[pl.ds((q ^ m) * rows, rows), :] = s[...]
    for cut in chunks(out_ref.shape[1], 4):
        out_ref[:, cut] = dot(inverse, p_ref[:, cut], NN, highest)
    own = pl.ds(pl.multiple_of(lax.axis_index("dp") * width, width), width)
    fix_ref[...] = dot(l_ref[:, rank : 2 * rank], w_ref[:, own], NN, highest)


def factor_kernel(t_ref, u_ref, l_ref, fix_ref, out_ref, z_ref, *, replicas):
    core = lax.axis_index("tensor") % 2
    half = t_ref.shape[0]
    rank = 2 * half
    z_ref[pl.ds(core * half, half), :] = t_ref[...]
    z_ref[pl.ds((1 - core) * half, half), :] = u_ref[...]
    inverse = l_ref[:, 2 * rank : 3 * rank] * (1.0 / replicas)
    out_ref[...] = dot(inverse, z_ref[...], NN, lax.Precision.HIGHEST) - fix_ref[...]


def call(kernel, outs, specs, scratch=(), flops=0, moved=0, vmem=32 << 20):
    return pl.pallas_call(
        kernel,
        out_shape=[jax.ShapeDtypeStruct(shape, F32) for shape in outs],
        in_specs=specs,
        out_specs=[VMEM_SPEC] * len(outs),
        scratch_shapes=scratch,
        compiler_params=pltpu.CompilerParams(vmem_limit_bytes=vmem),
        cost_estimate=pl.CostEstimate(flops=flops, bytes_accessed=moved, transcendentals=0),
    )


def swap_dp(x, m):
    n = lax.axis_size("dp")
    return lax.ppermute(x, "dp", [(i, i ^ m) for i in range(n)])


def swap_tensor(x, m):
    n = lax.axis_size("tensor")
    return lax.ppermute(x, "tensor", [(i, i ^ m) for i in range(n)])


def swap_both(x, md, mt):
    n, k = lax.axis_size("dp"), lax.axis_size("tensor")
    pairs = [(i * k + t, (i ^ md) * k + (t ^ mt)) for i in range(n) for t in range(k)]
    return lax.ppermute(x, ("dp", "tensor"), pairs)


def on_device(hidden, out_grad, prev_hidden, prev_grad, prev_basis, warm_start, *, norm_scale):
    replicas = lax.axis_size("dp")
    tokens, units = hidden.shape
    width = out_grad.shape[1]
    rank = warm_start.shape[1]
    rows, half, owned = rank // SQUARE, rank // 2, width // replicas
    w, b = warm_start.T, prev_basis.T
    piece = (rows, units)

    terms = call(
        left_factor_kernel,
        [piece] * SQUARE,
        [HBM_SPEC] * 5,
        [
            pltpu.VMEM((rank, width), F32),
            pltpu.VMEM((2 * tokens, width), BF16),
            pltpu.VMEM((2 * tokens, units), BF16),
            pltpu.SemaphoreType.DMA((20,)),
        ],
        flops=4 * tokens * rank * (units + width),
        moved=4 * tokens * (units + width) + 4 * rank * (units + width),
        vmem=60 << 20,
    )(w, out_grad, prev_grad, hidden, prev_hidden)
    got = [swap_dp(terms[m], m) for m in range(1, SQUARE)]
    (feedback,) = call(
        feedback_kernel,
        [piece],
        [VMEM_SPEC] * 2,
        [pltpu.VMEM((rank, rank), F32)],
        flops=2 * rank * rank * (units + width),
        moved=4 * rank * (units + width),
    )(w, b)
    summed = terms[0] + got[0] + got[1] + got[2]
    own = (summed + swap_dp(summed, SQUARE)) * (1.0 / replicas) - feedback
    p = [own] + [swap_dp(own, m) for m in range(1, SQUARE)]

    keep, send = call(
        pull_kernel,
        [(half, 2 * tokens)] * 2,
        [VMEM_SPEC] * 6,
        [pltpu.VMEM((rank, 2 * tokens), F32)],
        flops=8 * tokens * rank * units,
        moved=4 * tokens * units + 4 * rank * units,
    )(*p, hidden, prev_hidden)
    other = swap_tensor(send, 1)
    (gram,) = call(
        gram_kernel,
        [(rank, 128)],
        [VMEM_SPEC] * 5,
        [pltpu.VMEM((rank, units), F32)],
        flops=4 * rank * rank * units,
        moved=8 * rank * units,
    )(*p, b)
    parts = call(
        push_kernel,
        [(2, half, owned)] * SQUARE,
        [VMEM_SPEC] * 4 + [ANY_SPEC],
        flops=8 * tokens * half * width,
        moved=4 * tokens * width + 4 * half * width,
    )(keep, other, out_grad, prev_grad, gram)
    came = [swap_dp(parts[m], m) for m in range(1, SQUARE)]

    gram = gram + swap_tensor(gram, 1)
    gram = gram + swap_tensor(gram, 2)
    (solved,) = call(
        cholesky_kernel, [(rank, 128)], [VMEM_SPEC], flops=rank**3, moved=8 * rank * 128
    )(gram)
    near, far = call(
        near_far_kernel,
        [(half, owned)] * 2,
        [VMEM_SPEC] * 4 + [ANY_SPEC],
        flops=6 * half * owned,
        moved=40 * half * owned,
    )(parts[0], *came, solved)
    basis, fix = call(
        functools.partial(basis_kernel, norm_scale=norm_scale),
        [(rank, units), (rank, owned)],
        [VMEM_SPEC] * 6,
        [pltpu.VMEM((rank, units), F32)],
        flops=2 * rank * rank * units,
        moved=8 * rank * units,
    )(*p, solved, w)
    far_far, near_up, far_up = (
        swap_both(far, SQUARE, 2),
        swap_both(near, 0, 2),
        swap_both(far, SQUARE, 0),
    )
    (mine,) = call(
        total_kernel,
        [(half, owned)],
        [VMEM_SPEC] * 4 + [ANY_SPEC],
        flops=3 * half * owned,
        moved=20 * half * owned,
    )(near, far_far, near_up, far_up, fix)
    (factor,) = call(
        functools.partial(factor_kernel, replicas=replicas),
        [(rank, owned)],
        [VMEM_SPEC] * 4,
        [pltpu.VMEM((rank, owned), F32)],
        flops=2 * rank * rank * owned,
        moved=12 * rank * owned,
    )(mine, swap_tensor(mine, 1), solved, fix)
    return (basis.T, factor.T)


def fits(mesh, dp=8, tensor=4):
    return mesh.shape["dp"] == dp and mesh.shape["tensor"] == tensor


def solution(mesh):
    def whole(hidden, out_grad, prev_hidden, prev_grad, prev_basis, warm_start):
        norm_scale = float(prev_basis.shape[0]) ** 0.5
        body = on_device if fits(mesh) else plain_on_device
        return jax.shard_map(
            functools.partial(body, norm_scale=norm_scale),
            mesh=mesh,
            in_specs=(
                P("dp", "tensor"),
                P("dp", None),
                P("dp", "tensor"),
                P("dp", None),
                P("tensor", None),
                P(),
            ),
            out_specs=(P("tensor", None), P("dp", None)),
            check_vma=False,
        )(hidden, out_grad, prev_hidden, prev_grad, prev_basis, warm_start)

    return whole
```

```python
import functools

import jax
import jax.numpy as jnp
from jax import lax
from jax.experimental import pallas as pl
from jax.experimental.pallas import tpu as pltpu
from jax.sharding import PartitionSpec as P

F32 = jnp.float32
BF16 = jnp.bfloat16
SQUARE = 4
NT = (((1,), (1,)), ((), ()))
NN = (((1,), (0,)), ((), ()))
VMEM_SPEC = pl.BlockSpec(memory_space=pltpu.VMEM)
ANY_SPEC = pl.BlockSpec(memory_space=pl.ANY)
HBM_SPEC = pl.BlockSpec(memory_space=pltpu.HBM)


def orthonormal(rows_in, gram_matrix, norm_scale):
    lower = jnp.linalg.cholesky(gram_matrix)
    return norm_scale * jax.scipy.linalg.solve_triangular(lower, rows_in.T, lower=True).T


def plain_on_device(hidden, out_grad, prev_hidden, prev_grad, prev_basis, warm_start, *, norm_scale):
    highest = lax.Precision.HIGHEST
    replicas = lax.axis_size("dp")
    warm_low = warm_start.astype(BF16)
    projected = jnp.dot(out_grad, warm_low, preferred_element_type=F32).astype(BF16)
    projected_prev = jnp.dot(prev_grad, warm_low, preferred_element_type=F32).astype(BF16)
    coupling = jnp.dot(warm_start.T, warm_start, precision=highest)
    summed = jnp.einsum("tf,tr->fr", hidden, projected, preferred_element_type=F32)
    summed = summed + jnp.einsum(
        "tf,tr->fr", prev_hidden, projected_prev, preferred_element_type=F32
    )
    local_p = (summed - jnp.dot(prev_basis, coupling, precision=highest)) / replicas
    p_mean = lax.psum(local_p, "dp")
    gram_matrix = lax.psum(jnp.dot(p_mean.T, p_mean, precision=highest), "tensor")
    new_basis = orthonormal(p_mean, gram_matrix, norm_scale)
    basis_low = new_basis.astype(BF16)
    pulled = jnp.dot(hidden, basis_low, preferred_element_type=F32).astype(BF16)
    pulled_prev = jnp.dot(prev_hidden, basis_low, preferred_element_type=F32).astype(BF16)
    cross_basis = jnp.dot(prev_basis.T, new_basis, precision=highest)
    summed_q = jnp.einsum("td,tr->dr", out_grad, pulled, preferred_element_type=F32)
    summed_q = summed_q + jnp.einsum(
        "td,tr->dr", prev_grad, pulled_prev, preferred_element_type=F32
    )
    local_q = (summed_q - jnp.dot(warm_start, cross_basis, precision=highest)) / replicas
    row_count = warm_start.shape[0] // replicas
    summed_all = lax.psum(local_q, ("dp", "tensor"))
    owned_rows = lax.dynamic_slice_in_dim(
        summed_all, lax.axis_index("dp") * row_count, row_count, 0
    )
    return (new_basis, owned_rows / norm_scale)


def split(x, terms):
    parts = []
    for i in range(terms):
        part = x.astype(BF16)
        parts.append(part)
        if i + 1 < terms:
            x = x - part.astype(F32)
    return parts


def dot(a, b, dims, precision=None):
    return lax.dot_general(a, b, dims, preferred_element_type=F32, precision=precision)


def chunks(extent, count):
    step = extent // count
    return [pl.ds(i * step, step) for i in range(count)]


def store_pieces(pieces, cut, summed):
    rows = pieces[0].shape[0]
    for m, piece in enumerate(pieces):
        piece[:, cut] = summed[m * rows : (m + 1) * rows]


def first_term_kernel(w_ref, o_ref, o2_ref, h_ref, h2_ref, *refs):
    pieces, y_ref, (wv, ov, hv, sem) = refs[:SQUARE], refs[SQUARE], refs[SQUARE + 1 :]
    q = lax.axis_index("dp") % SQUARE
    rows = wv.shape[0] // SQUARE
    tokens = o_ref.shape[0]
    o_cuts, h_cuts = chunks(o_ref.shape[1], 4), chunks(hv.shape[1], 2)
    copies = []
    for m in range(SQUARE):
        copies.append(
            pltpu.make_async_copy(
                w_ref.at[pl.ds((q ^ m) * rows, rows), :], wv.at[pl.ds(m * rows, rows), :], sem.at[m]
            )
        )
    for i, cut in enumerate(o_cuts):
        for j, ref in enumerate((o_ref, o2_ref)):
            copies.append(
                pltpu.make_async_copy(
                    ref.at[:, cut], ov.at[pl.ds(j * tokens, tokens), cut], sem.at[4 + 2 * i + j]
                )
            )
    for i, cut in enumerate(h_cuts):
        for j, ref in enumerate((h_ref, h2_ref)):
            copies.append(
                pltpu.make_async_copy(
                    ref.at[:, cut], hv.at[pl.ds(j * tokens, tokens), cut], sem.at[12 + 2 * i + j]
                )
            )
    for copy in copies:
        copy.start()
    for copy in copies[:4]:
        copy.wait()
    projected = jnp.zeros((wv.shape[0], 2 * tokens), F32)
    for i, cut in enumerate(o_cuts):
        copies[4 + 2 * i].wait()
        copies[5 + 2 * i].wait()
        projected += dot(wv[:, cut].astype(BF16), ov[:, cut], NT)
    projected = projected.astype(BF16)
    y_ref[...] = projected.astype(F32)
    for i, cut in enumerate(h_cuts):
        copies[12 + 2 * i].wait()
        copies[13 + 2 * i].wait()
        store_pieces(pieces, cut, dot(projected, hv[:, cut], NN))


def second_term_kernel(y_ref, h_ref, h2_ref, *refs):
    pieces, (hv, sem) = refs[:SQUARE], refs[SQUARE:]
    tokens, units = h_ref.shape
    first = units - hv.shape[1]
    cuts = chunks(hv.shape[1], 2)
    copies = []
    for i, cut in enumerate(cuts):
        for j, ref in enumerate((h_ref, h2_ref)):
            copies.append(
                pltpu.make_async_copy(
                    ref.at[:, pl.ds(first + cut.start, cut.size)],
                    hv.at[pl.ds(j * tokens, tokens), cut],
                    sem.at[2 * i + j],
                )
            )
    for copy in copies:
        copy.start()
    projected = y_ref[...].astype(BF16)
    for i, cut in enumerate(cuts):
        copies[2 * i].wait()
        copies[2 * i + 1].wait()
        store_pieces(pieces, cut, dot(projected, hv[:, cut], NN))


def feedback_kernel(w_ref, b_ref, out_ref, c_ref):
    q = lax.axis_index("dp") % SQUARE
    rows = out_ref.shape[0]
    rank = w_ref.shape[0]
    total = jnp.zeros((3 * rank, 3 * rank), F32)
    for cut in chunks(w_ref.shape[1], 4):
        stacked = jnp.concatenate(split(w_ref[:, cut], 3), axis=0)
        total += dot(stacked, stacked, NT)
    total = total[:rank] + total[rank : 2 * rank] + total[2 * rank :]
    c_ref[...] = total[:, :rank] + total[:, rank : 2 * rank] + total[:, 2 * rank :]
    own = c_ref[pl.ds(q * rows, rows), :]
    for cut in chunks(b_ref.shape[1], 4):
        out_ref[:, cut] = dot(own, b_ref[:, cut], NN, lax.Precision.HIGHEST)


def pulled_rows(pieces, h_ref, h2_ref, cuts):
    rank, tokens = SQUARE * pieces[0].shape[0], h_ref.shape[0]
    now = jnp.zeros((2 * rank, tokens), F32)
    prev = jnp.zeros((2 * rank, tokens), F32)
    for cut, units in cuts:
        p = jnp.concatenate([s[:, cut] for s in pieces], axis=0)
        stacked = jnp.concatenate(split(p, 2), axis=0)
        now += dot(stacked, h_ref[:, units], NT)
        prev += dot(stacked, h2_ref[:, units], NT)
    both = jnp.concatenate([now, prev], axis=1)
    return both[:rank] + both[rank:]


def cuts_of(pieces, first, count):
    cuts = chunks(pieces[0].shape[1], count)
    return [(cut, pl.ds(first + cut.start, cut.size)) for cut in cuts]


def first_pull_kernel(s0, s1, s2, s3, h_ref, h2_ref, b_ref, v_ref, g_ref, p_ref):
    pieces = (s0, s1, s2, s3)
    cuts = cuts_of(pieces, 0, 2)
    v_ref[...] = pulled_rows(pieces, h_ref, h2_ref, cuts)
    g_ref[...] = gram_terms(pieces, b_ref, p_ref, cuts)


def pull_kernel(s0, s1, s2, s3, first_ref, h_ref, h2_ref, keep_ref, send_ref, v_ref):
    q = lax.axis_index("dp") % SQUARE
    core = lax.axis_index("tensor") % 2
    pieces = (s0, s1, s2, s3)
    rows, half = s0.shape[0], keep_ref.shape[0]
    first = h_ref.shape[1] - s0.shape[1]
    both = first_ref[...] + pulled_rows(pieces, h_ref, h2_ref, cuts_of(pieces, first, 2))
    for m in range(SQUARE):
        v_ref[pl.ds((q ^ m) * rows, rows), :] = both[m * rows : (m + 1) * rows]
    keep_ref[...] = v_ref[pl.ds(core * half, half), :]
    send_ref[...] = v_ref[pl.ds((1 - core) * half, half), :]


def ordered(pieces, p_ref):
    q = lax.axis_index("dp") % SQUARE
    rows = pieces[0].shape[0]
    for m, s in enumerate(pieces):
        p_ref[pl.ds((q ^ m) * rows, rows), :] = s[...]


def gram_terms(pieces, b_ref, p_ref, cuts):
    ordered(pieces, p_ref)
    rank = SQUARE * pieces[0].shape[0]
    total = jnp.zeros((3 * rank, 6 * rank), F32)
    for cut, units in cuts:
        p = split(p_ref[:, cut], 3)
        b = split(b_ref[:, units], 3)
        total += dot(jnp.concatenate(p, axis=0), jnp.concatenate(p + b, axis=0), NT)
    total = total[:rank] + total[rank : 2 * rank] + total[2 * rank :]
    gram = total[:, :rank] + total[:, rank : 2 * rank] + total[:, 2 * rank : 3 * rank]
    cross = total[:, 3 * rank : 4 * rank] + total[:, 4 * rank : 5 * rank] + total[:, 5 * rank :]
    return jnp.concatenate([gram, cross, jnp.zeros((rank, 128 - 2 * rank), F32)], axis=1)


def gram_kernel(s0, s1, s2, s3, b_ref, first_ref, out_ref, p_ref):
    pieces = (s0, s1, s2, s3)
    first = b_ref.shape[1] - s0.shape[1]
    out_ref[...] = first_ref[...] + gram_terms(pieces, b_ref, p_ref, cuts_of(pieces, first, 2))


def push_kernel(mine_ref, got_ref, o_ref, o2_ref, after_ref, *outs):
    me = lax.axis_index("dp")
    tokens = o_ref.shape[0]
    half, width = outs[0].shape[1:]
    v = jnp.concatenate(split(mine_ref[...] + got_ref[...], 2), axis=0)
    for m in range(SQUARE):
        for z in range(2):
            cut = pl.ds(pl.multiple_of((me ^ m ^ (SQUARE * z)) * width, width), width)
            both = dot(v[:, :tokens], o_ref[:, cut], NN) + dot(v[:, tokens:], o2_ref[:, cut], NN)
            outs[m][z] = both[:half] + both[half:]


def cholesky_kernel(in_ref, out_ref):
    rank = in_ref.shape[0]
    shape = in_ref.shape
    row = lax.broadcasted_iota(jnp.int32, shape, 0)
    lane = lax.broadcasted_iota(jnp.int32, shape, 1)
    a = jnp.where(lane == row + 2 * rank, 1.0, in_ref[...])
    for k in range(rank):
        pivot = a[k : k + 1, k : k + 1]
        scale = 1.0 / jnp.sqrt(pivot)
        top = a[k : k + 1, :] * scale
        below = jnp.where(row[:, :1] > k, a[:, k : k + 1] * scale, 0.0)
        a = jnp.where(row == k, top, a - below * top)
    out_ref[...] = a


def near_far_kernel(a_ref, b_ref, c_ref, d_ref, after_ref, near_ref, far_ref):
    near_ref[...] = a_ref[0] + b_ref[0] + c_ref[0] + d_ref[0]
    far_ref[...] = a_ref[1] + b_ref[1] + c_ref[1] + d_ref[1]


def total_kernel(a_ref, b_ref, after_ref, out_ref):
    out_ref[...] = a_ref[...] + b_ref[...]


def basis_kernel(u0, u1, u2, u3, s0, s1, s2, s3, l_ref, w_ref, out_ref, fix_ref, p_ref, r_ref, *, norm_scale):
    rank = l_ref.shape[0]
    width = fix_ref.shape[1]
    highest = lax.Precision.HIGHEST
    inverse = l_ref[:, 2 * rank : 3 * rank] * norm_scale
    first = 0
    for pieces, ref in (((u0, u1, u2, u3), p_ref), ((s0, s1, s2, s3), r_ref)):
        ordered(pieces, ref)
        for cut, units in cuts_of(pieces, first, 2):
            out_ref[:, units] = dot(inverse, ref[:, cut], NN, highest)
        first += ref.shape[1]
    own = pl.ds(pl.multiple_of(lax.axis_index("dp") * width, width), width)
    fix_ref[...] = dot(l_ref[:, rank : 2 * rank], w_ref[:, own], NN, highest)


def factor_kernel(t_ref, u_ref, l_ref, fix_ref, out_ref, z_ref, *, replicas):
    core = lax.axis_index("tensor") % 2
    half = t_ref.shape[0]
    rank = 2 * half
    z_ref[pl.ds(core * half, half), :] = t_ref[...]
    z_ref[pl.ds((1 - core) * half, half), :] = u_ref[...]
    inverse = l_ref[:, 2 * rank : 3 * rank] * (1.0 / replicas)
    out_ref[...] = dot(inverse, z_ref[...], NN, lax.Precision.HIGHEST) - fix_ref[...]


def call(kernel, outs, specs, scratch=(), flops=0, moved=0, vmem=32 << 20):
    return pl.pallas_call(
        kernel,
        out_shape=[jax.ShapeDtypeStruct(shape, F32) for shape in outs],
        in_specs=specs,
        out_specs=[VMEM_SPEC] * len(outs),
        scratch_shapes=scratch,
        compiler_params=pltpu.CompilerParams(vmem_limit_bytes=vmem),
        cost_estimate=pl.CostEstimate(flops=flops, bytes_accessed=moved, transcendentals=0),
    )


def in_hbm(x):
    return pltpu.with_memory_space_constraint(x, pltpu.HBM)


def swap_dp(x, m):
    n = lax.axis_size("dp")
    return lax.ppermute(x, "dp", [(i, i ^ m) for i in range(n)])


def swap_tensor(x, m):
    n = lax.axis_size("tensor")
    return lax.ppermute(x, "tensor", [(i, i ^ m) for i in range(n)])


def on_device(hidden, out_grad, prev_hidden, prev_grad, prev_basis, warm_start, *, norm_scale):
    replicas = lax.axis_size("dp")
    tokens, units = hidden.shape
    width = out_grad.shape[1]
    rank = warm_start.shape[1]
    rows, half, owned = rank // SQUARE, rank // 2, width // replicas
    w, b = warm_start.T, prev_basis.T
    first = units // 256 * 128
    rest = units - first

    *terms, projected = call(
        first_term_kernel,
        [(rows, first)] * SQUARE + [(rank, 2 * tokens)],
        [HBM_SPEC] * 5,
        [
            pltpu.VMEM((rank, width), F32),
            pltpu.VMEM((2 * tokens, width), BF16),
            pltpu.VMEM((2 * tokens, first), BF16),
            pltpu.SemaphoreType.DMA((16,)),
        ],
        flops=4 * tokens * rank * (first + width),
        moved=4 * tokens * (first + width) + 4 * rank * (first + width),
    )(*[in_hbm(x) for x in (w, out_grad, prev_grad, hidden, prev_hidden)])
    late_terms = call(
        second_term_kernel,
        [(rows, rest)] * SQUARE,
        [VMEM_SPEC] + [HBM_SPEC] * 2,
        [pltpu.VMEM((2 * tokens, rest), BF16), pltpu.SemaphoreType.DMA((4,))],
        flops=4 * tokens * rank * rest,
        moved=4 * tokens * rest + 4 * rank * rest,
    )(projected, in_hbm(hidden), in_hbm(prev_hidden))
    (feedback,) = call(
        feedback_kernel,
        [(rows, units)],
        [VMEM_SPEC] * 2,
        [pltpu.VMEM((rank, rank), F32)],
        flops=2 * rank * rank * (units + width),
        moved=4 * rank * (units + width),
    )(w, b)

    def swap_square(x):
        return [swap_dp(x[m], m) for m in range(1, SQUARE)]

    def mean(summed, came, correction):
        return (summed + came) * (1.0 / replicas) - correction

    early = terms[0] + sum(swap_square(terms))
    early_came = swap_dp(early, SQUARE)
    late = late_terms[0] + sum(swap_square(late_terms))
    late_came = swap_dp(late, SQUARE)
    early_own = mean(early, early_came, feedback[:, :first])
    early_p = [early_own] + swap_square([early_own] * SQUARE)
    late_own = mean(late, late_came, feedback[:, first:])
    late_p = [late_own] + swap_square([late_own] * SQUARE)

    early_v, early_gram = call(
        first_pull_kernel,
        [(rank, 2 * tokens), (rank, 128)],
        [VMEM_SPEC] * 7,
        [pltpu.VMEM((rank, first), F32)],
        flops=8 * tokens * rank * first,
        moved=4 * tokens * first + 4 * rank * first,
    )(*early_p, hidden, prev_hidden, b)
    keep, send = call(
        pull_kernel,
        [(half, 2 * tokens)] * 2,
        [VMEM_SPEC] * 7,
        [pltpu.VMEM((rank, 2 * tokens), F32)],
        flops=8 * tokens * rank * rest,
        moved=4 * tokens * rest + 4 * rank * rest,
    )(*late_p, early_v, hidden, prev_hidden)
    other = swap_tensor(send, 1)
    (gram,) = call(
        gram_kernel,
        [(rank, 128)],
        [VMEM_SPEC] * 6,
        [pltpu.VMEM((rank, rest), F32)],
        flops=4 * rank * rank * rest,
        moved=8 * rank * rest,
    )(*late_p, b, early_gram)
    gram_came = swap_tensor(gram, 1)
    plane = keep + other
    plane_came = swap_tensor(plane, 2)
    gram = gram + gram_came
    parts = call(
        push_kernel,
        [(2, half, owned)] * SQUARE,
        [VMEM_SPEC] * 4 + [ANY_SPEC],
        flops=8 * tokens * half * width,
        moved=4 * tokens * width + 4 * half * width,
    )(plane, plane_came, out_grad, prev_grad, gram)
    came = swap_square(parts)
    gram = gram + swap_tensor(gram, 2)
    (solved,) = call(
        cholesky_kernel, [(rank, 128)], [VMEM_SPEC], flops=rank**3, moved=8 * rank * 128
    )(gram)
    near, far = call(
        near_far_kernel,
        [(half, owned)] * 2,
        [VMEM_SPEC] * 4 + [ANY_SPEC],
        flops=6 * half * owned,
        moved=40 * half * owned,
    )(parts[0], *came, solved)
    basis, fix = call(
        functools.partial(basis_kernel, norm_scale=norm_scale),
        [(rank, units), (rank, owned)],
        [VMEM_SPEC] * 10,
        [pltpu.VMEM((rank, first), F32), pltpu.VMEM((rank, rest), F32)],
        flops=2 * rank * rank * units,
        moved=8 * rank * units,
    )(*early_p, *late_p, solved, w)
    (mine,) = call(
        total_kernel,
        [(half, owned)],
        [VMEM_SPEC] * 2 + [ANY_SPEC],
        flops=half * owned,
        moved=12 * half * owned,
    )(near, swap_dp(far, SQUARE), fix)
    (factor,) = call(
        functools.partial(factor_kernel, replicas=replicas),
        [(rank, owned)],
        [VMEM_SPEC] * 4,
        [pltpu.VMEM((rank, owned), F32)],
        flops=2 * rank * rank * owned,
        moved=12 * rank * owned,
    )(mine, swap_tensor(mine, 1), solved, fix)
    return (basis.T, factor.T)


def fits(mesh, dp=8, tensor=4):
    return mesh.shape["dp"] == dp and mesh.shape["tensor"] == tensor


def solution(mesh):
    def whole(hidden, out_grad, prev_hidden, prev_grad, prev_basis, warm_start):
        norm_scale = float(prev_basis.shape[0]) ** 0.5
        body = on_device if fits(mesh) else plain_on_device
        return jax.shard_map(
            functools.partial(body, norm_scale=norm_scale),
            mesh=mesh,
            in_specs=(
                P("dp", "tensor"),
                P("dp", None),
                P("dp", "tensor"),
                P("dp", None),
                P("tensor", None),
                P(),
            ),
            out_specs=(P("tensor", None), P("dp", None)),
            check_vma=False,
        )(hidden, out_grad, prev_hidden, prev_grad, prev_basis, warm_start)

    return whole
```

```python
import functools

import jax
import jax.numpy as jnp
from jax import lax
from jax.experimental import pallas as pl
from jax.experimental.pallas import tpu as pltpu
from jax.sharding import PartitionSpec as P

F32 = jnp.float32
BF16 = jnp.bfloat16
SQUARE = 4
TERMS_AWAY = (0, 3, 2, 1)
SUMS_AWAY = (0, 3, 2, 1)
RIGHT_AWAY = (0, 3, 2, 1)
NT = (((1,), (1,)), ((), ()))
NN = (((1,), (0,)), ((), ()))
VMEM_SPEC = pl.BlockSpec(memory_space=pltpu.VMEM)
ANY_SPEC = pl.BlockSpec(memory_space=pl.ANY)
HBM_SPEC = pl.BlockSpec(memory_space=pltpu.HBM)


def orthonormal(rows_in, gram_matrix, norm_scale):
    lower = jnp.linalg.cholesky(gram_matrix)
    return norm_scale * jax.scipy.linalg.solve_triangular(lower, rows_in.T, lower=True).T


def plain_on_device(hidden, out_grad, prev_hidden, prev_grad, prev_basis, warm_start, *, norm_scale):
    highest = lax.Precision.HIGHEST
    replicas = lax.axis_size("dp")
    warm_low = warm_start.astype(BF16)
    projected = jnp.dot(out_grad, warm_low, preferred_element_type=F32).astype(BF16)
    projected_prev = jnp.dot(prev_grad, warm_low, preferred_element_type=F32).astype(BF16)
    coupling = jnp.dot(warm_start.T, warm_start, precision=highest)
    summed = jnp.einsum("tf,tr->fr", hidden, projected, preferred_element_type=F32)
    summed = summed + jnp.einsum(
        "tf,tr->fr", prev_hidden, projected_prev, preferred_element_type=F32
    )
    local_p = (summed - jnp.dot(prev_basis, coupling, precision=highest)) / replicas
    p_mean = lax.psum(local_p, "dp")
    gram_matrix = lax.psum(jnp.dot(p_mean.T, p_mean, precision=highest), "tensor")
    new_basis = orthonormal(p_mean, gram_matrix, norm_scale)
    basis_low = new_basis.astype(BF16)
    pulled = jnp.dot(hidden, basis_low, preferred_element_type=F32).astype(BF16)
    pulled_prev = jnp.dot(prev_hidden, basis_low, preferred_element_type=F32).astype(BF16)
    cross_basis = jnp.dot(prev_basis.T, new_basis, precision=highest)
    summed_q = jnp.einsum("td,tr->dr", out_grad, pulled, preferred_element_type=F32)
    summed_q = summed_q + jnp.einsum(
        "td,tr->dr", prev_grad, pulled_prev, preferred_element_type=F32
    )
    local_q = (summed_q - jnp.dot(warm_start, cross_basis, precision=highest)) / replicas
    row_count = warm_start.shape[0] // replicas
    summed_all = lax.psum(local_q, ("dp", "tensor"))
    owned_rows = lax.dynamic_slice_in_dim(
        summed_all, lax.axis_index("dp") * row_count, row_count, 0
    )
    return (new_basis, owned_rows / norm_scale)


def split(x, terms):
    parts = []
    for i in range(terms):
        part = x.astype(BF16)
        parts.append(part)
        if i + 1 < terms:
            x = x - part.astype(F32)
    return parts


def dot(a, b, dims, precision=None):
    return lax.dot_general(a, b, dims, preferred_element_type=F32, precision=precision)


def chunks(extent, count):
    step = extent // count
    return [pl.ds(i * step, step) for i in range(count)]


def store_pieces(pieces, cut, summed):
    rows = pieces[0].shape[0]
    for i, piece in enumerate(pieces):
        piece[:, cut] = summed[i * rows : (i + 1) * rows]


def first_term_kernel(w_ref, o_ref, o2_ref, h_ref, h2_ref, *refs):
    pieces, (y_ref, ov, hv, wv, sem) = refs[:SQUARE], refs[SQUARE:]
    q = lax.axis_index("dp") % SQUARE
    rows = wv.shape[0] // SQUARE
    tokens = o_ref.shape[0]
    first = pieces[0].shape[1]
    copies = []

    def copy(source, target):
        copies.append(pltpu.make_async_copy(source, target, sem.at[len(copies)]))
        copies[-1].start()
        return copies[-1]

    def stacked(cut, ref, ref2, target):
        return [
            copy(r.at[:, cut], target.at[pl.ds(j * tokens, tokens), cut]) for j, r in enumerate((ref, ref2))
        ]

    def wait(pending):
        for c in pending:
            c.wait()

    o_cuts, h_cuts = chunks(o_ref.shape[1], 4), chunks(first, 2)
    w_copies = [
        copy(w_ref.at[pl.ds((q ^ m) * rows, rows), :], wv.at[pl.ds(i * rows, rows), :])
        for i, m in enumerate(TERMS_AWAY)
    ]
    o_copies = [stacked(cut, o_ref, o2_ref, ov) for cut in o_cuts]
    h_copies = [stacked(cut, h_ref, h2_ref, hv) for cut in h_cuts]
    wait(w_copies)
    projected = jnp.zeros((wv.shape[0], 2 * tokens), F32)
    for i, cut in enumerate(o_cuts):
        wait(o_copies[i])
        projected += dot(wv[:, cut].astype(BF16), ov[:, cut], NT)
    rest = stacked(pl.ds(first, h_ref.shape[1] - first), h_ref, h2_ref, hv)
    y_ref[...] = projected
    projected = projected.astype(BF16)
    for i, cut in enumerate(h_cuts):
        wait(h_copies[i])
        store_pieces(pieces, cut, dot(projected, hv[:, cut], NN))
    wait(rest)


def second_term_kernel(y_ref, h_ref, *pieces):
    first = h_ref.shape[1] - pieces[0].shape[1]
    projected = y_ref[...].astype(BF16)
    for cut, units in cuts_of(pieces, first, 2):
        store_pieces(pieces, cut, dot(projected, h_ref[:, units], NN))


def feedback_kernel(w_ref, b_ref, after_ref, first_ref, rest_ref, c_ref):
    q = lax.axis_index("dp") % SQUARE
    rank = w_ref.shape[0]
    rows = rank // SQUARE
    total = jnp.zeros((3 * rank, 3 * rank), F32)
    for cut in chunks(w_ref.shape[1], 4):
        terms = jnp.concatenate(split(w_ref[:, cut], 3), axis=0)
        total += dot(terms, terms, NT)
    total = total[:rank] + total[rank : 2 * rank] + total[2 * rank :]
    c_ref[...] = total[:, :rank] + total[:, rank : 2 * rank] + total[:, 2 * rank :]
    coupling = jnp.concatenate(
        [c_ref[pl.ds((q ^ m) * rows, rows), :] for m in SUMS_AWAY], axis=0
    )
    first = 0
    for ref in (first_ref, rest_ref):
        for cut, units in cuts_of((ref,), first, 2):
            ref[:, cut] = dot(coupling, b_ref[:, units], NN, lax.Precision.HIGHEST)
        first += ref.shape[1]


def products(pieces, f_ref, h_ref, b_ref, p_ref, first):
    q = lax.axis_index("dp") % SQUARE
    rows = pieces[0].shape[0]
    rank = SQUARE * rows
    pulled = jnp.zeros((2 * rank, h_ref.shape[0]), F32)
    total = jnp.zeros((3 * rank, 6 * rank), F32)
    for cut, units in cuts_of(pieces, first, 2):
        p = jnp.concatenate([s[:, cut] for s in pieces], axis=0) - f_ref[:, cut]
        for i, m in enumerate(SUMS_AWAY):
            p_ref[pl.ds((q ^ m) * rows, rows), cut] = p[i * rows : (i + 1) * rows]
        pulled += dot(jnp.concatenate(split(p, 2), axis=0), h_ref[:, units], NT)
    for cut, units in cuts_of(pieces, first, 2):
        p = split(p_ref[:, cut], 3)
        b = split(b_ref[:, units], 3)
        total += dot(jnp.concatenate(p, axis=0), jnp.concatenate(p + b, axis=0), NT)
    pulled = pulled[:rank] + pulled[rank:]
    total = total[:rank] + total[rank : 2 * rank] + total[2 * rank :]
    gram = total[:, :rank] + total[:, rank : 2 * rank] + total[:, 2 * rank : 3 * rank]
    cross = total[:, 3 * rank : 4 * rank] + total[:, 4 * rank : 5 * rank] + total[:, 5 * rank :]
    grams = jnp.concatenate([gram, cross, jnp.zeros((rank, 128 - 2 * rank), F32)], axis=1)
    return pulled, grams


def cuts_of(pieces, first, count):
    cuts = chunks(pieces[0].shape[1], count)
    return [(cut, pl.ds(first + cut.start, cut.size)) for cut in cuts]


def first_pull_kernel(s0, s1, s2, s3, f_ref, h_ref, b_ref, p_ref, v_ref, g_ref):
    v_ref[...], g_ref[...] = products((s0, s1, s2, s3), f_ref, h_ref, b_ref, p_ref, 0)


def pull_kernel(s0, s1, s2, s3, f_ref, h_ref, b_ref, v_ref, g_ref, p_ref, keep_ref, send_ref, t_ref):
    q = lax.axis_index("dp") % SQUARE
    core = lax.axis_index("tensor") % 2
    rows, half, tokens = s0.shape[0], keep_ref.shape[0], h_ref.shape[0]
    first = h_ref.shape[1] - s0.shape[1]
    pulled, grams = products((s0, s1, s2, s3), f_ref, h_ref, b_ref, p_ref, first)
    pulled += v_ref[...]
    grams += g_ref[...]
    for i, m in enumerate(SUMS_AWAY):
        t_ref[pl.ds((q ^ m) * rows, rows), :] = pulled[i * rows : (i + 1) * rows]
    keep_ref[:, :tokens] = t_ref[pl.ds(core * half, half), :]
    send_ref[:, :tokens] = t_ref[pl.ds((1 - core) * half, half), :]
    for ref in (keep_ref, send_ref):
        ref[:, tokens : tokens + 128] = grams[:half]
        ref[:, tokens + 128 :] = grams[half:]


def push_kernel(mine_ref, got_ref, o_ref, *outs):
    me = lax.axis_index("dp")
    tokens = o_ref.shape[0]
    half, width = outs[0].shape[1:]
    v = jnp.concatenate(split(mine_ref[:, :tokens] + got_ref[:, :tokens], 2), axis=0)
    for i, m in enumerate(RIGHT_AWAY):
        for z in range(2):
            cut = pl.ds(pl.multiple_of((me ^ m ^ (SQUARE * z)) * width, width), width)
            both = dot(v, o_ref[:, cut], NN)
            outs[i][z] = both[:half] + both[half:]


def cholesky_kernel(mine_ref, got_ref, out_ref):
    rank, lanes = out_ref.shape
    shape = out_ref.shape
    tokens = mine_ref.shape[1] - 2 * lanes
    grams = mine_ref[:, tokens:] + got_ref[:, tokens:]
    grams = jnp.concatenate([grams[:, :lanes], grams[:, lanes:]], axis=0)
    row = lax.broadcasted_iota(jnp.int32, shape, 0)
    lane = lax.broadcasted_iota(jnp.int32, shape, 1)
    a = jnp.where(lane == row + 2 * rank, 1.0, grams)
    for k in range(rank):
        pivot = a[k : k + 1, k : k + 1]
        scale = 1.0 / jnp.sqrt(pivot)
        top = a[k : k + 1, :] * scale
        below = jnp.where(row[:, :1] > k, a[:, k : k + 1] * scale, 0.0)
        a = jnp.where(row == k, top, a - below * top)
    out_ref[...] = a


def near_far_kernel(a_ref, b_ref, c_ref, d_ref, after_ref, near_ref, far_ref):
    near_ref[...] = a_ref[0] + b_ref[0] + c_ref[0] + d_ref[0]
    far_ref[...] = a_ref[1] + b_ref[1] + c_ref[1] + d_ref[1]


def total_kernel(a_ref, b_ref, after_ref, out_ref):
    out_ref[...] = a_ref[...] + b_ref[...]


def basis_kernel(p_ref, r_ref, l_ref, w_ref, out_ref, fix_ref, *, norm_scale):
    rank = l_ref.shape[0]
    width = fix_ref.shape[1]
    highest = lax.Precision.HIGHEST
    inverse = l_ref[:, 2 * rank : 3 * rank] * norm_scale
    first = 0
    for ref in (p_ref, r_ref):
        for cut, units in cuts_of((ref,), first, 2):
            out_ref[:, units] = dot(inverse, ref[:, cut], NN, highest)
        first += ref.shape[1]
    own = pl.ds(pl.multiple_of(lax.axis_index("dp") * width, width), width)
    fix_ref[...] = dot(l_ref[:, rank : 2 * rank], w_ref[:, own], NN, highest)


def factor_kernel(t_ref, u_ref, l_ref, fix_ref, out_ref, z_ref, *, replicas):
    core = lax.axis_index("tensor") % 2
    half = t_ref.shape[0]
    rank = 2 * half
    z_ref[pl.ds(core * half, half), :] = t_ref[...]
    z_ref[pl.ds((1 - core) * half, half), :] = u_ref[...]
    inverse = l_ref[:, 2 * rank : 3 * rank] * (1.0 / replicas)
    out_ref[...] = dot(inverse, z_ref[...], NN, lax.Precision.HIGHEST) - fix_ref[...]


def call(kernel, outs, specs, scratch=(), flops=0, moved=0, vmem=32 << 20):
    return pl.pallas_call(
        kernel,
        out_shape=[jax.ShapeDtypeStruct(shape[:2] if BF16 in shape else shape, BF16 if BF16 in shape else F32) for shape in outs],
        in_specs=specs,
        out_specs=[VMEM_SPEC] * len(outs),
        scratch_shapes=scratch,
        compiler_params=pltpu.CompilerParams(vmem_limit_bytes=vmem),
        cost_estimate=pl.CostEstimate(flops=flops, bytes_accessed=moved, transcendentals=0),
    )


def in_hbm(x):
    return pltpu.with_memory_space_constraint(x, pltpu.HBM)


def swap_dp(x, m):
    n = lax.axis_size("dp")
    return lax.ppermute(x, "dp", [(i, i ^ m) for i in range(n)])


def swap_tensor(x, m):
    n = lax.axis_size("tensor")
    return lax.ppermute(x, "tensor", [(i, i ^ m) for i in range(n)])


def on_device(hidden, out_grad, prev_hidden, prev_grad, prev_basis, warm_start, *, norm_scale):
    replicas = lax.axis_size("dp")
    tokens, units = hidden.shape
    width = out_grad.shape[1]
    rank = warm_start.shape[1]
    rows, half, owned = rank // SQUARE, rank // 2, width // replicas
    w, b = warm_start.T, prev_basis.T
    first = units // 256 * 128
    rest = units - first

    *terms, projected, out_grads, hiddens = call(
        first_term_kernel,
        [(rows, first)] * SQUARE + [(rank, 2 * tokens), (2 * tokens, width, BF16), (2 * tokens, units, BF16)],
        [HBM_SPEC] * 5,
        [pltpu.VMEM((rank, width), F32), pltpu.SemaphoreType.DMA((18,))],
        flops=4 * tokens * rank * (first + width),
        moved=4 * tokens * (units + width) + 4 * rank * (first + width),
    )(*[in_hbm(x) for x in (w, out_grad, prev_grad, hidden, prev_hidden)])
    late_terms = call(
        second_term_kernel,
        [(rows, rest)] * SQUARE,
        [VMEM_SPEC] * 2,
        flops=4 * tokens * rank * rest,
        moved=4 * tokens * rest + 4 * rank * rest,
    )(projected, hiddens)

    def swap_square(x, away):
        return [swap_dp(x[i], m) for i, m in enumerate(away) if m]

    def mean(summed, came):
        own = (summed + came) * (1.0 / replicas)
        return [own] + swap_square([own] * SQUARE, SUMS_AWAY)

    early = terms[0] + sum(swap_square(terms, TERMS_AWAY))
    early_came = swap_dp(early, SQUARE)
    late = late_terms[0] + sum(swap_square(late_terms, TERMS_AWAY))
    late_came = swap_dp(late, SQUARE)
    early_feedback, late_feedback = call(
        feedback_kernel,
        [(rank, first), (rank, rest)],
        [VMEM_SPEC] * 2 + [ANY_SPEC],
        [pltpu.VMEM((rank, rank), F32)],
        flops=2 * rank * rank * (units + width),
        moved=4 * rank * (units + width),
    )(w, b, late)
    early_came, early_feedback = lax.optimization_barrier((early_came, early_feedback))
    early_p = mean(early, early_came)
    late_p = mean(late, late_came)

    p_first, early_v, early_gram = call(
        first_pull_kernel,
        [(rank, first), (rank, 2 * tokens), (rank, 128)],
        [VMEM_SPEC] * 7,
        flops=8 * tokens * rank * first,
        moved=4 * tokens * first + 4 * rank * first,
    )(*early_p, early_feedback, hiddens, b)
    p_rest, keep, send = call(
        pull_kernel,
        [(rank, rest)] + [(half, 2 * tokens + 256)] * 2,
        [VMEM_SPEC] * 9,
        [pltpu.VMEM((rank, 2 * tokens), F32)],
        flops=8 * tokens * rank * rest,
        moved=4 * tokens * rest + 4 * rank * rest,
    )(*late_p, late_feedback, hiddens, b, early_v, early_gram)
    plane = keep + swap_tensor(send, 1)
    plane_came = swap_tensor(plane, 2)
    parts = call(
        push_kernel,
        [(2, half, owned)] * SQUARE,
        [VMEM_SPEC] * 3,
        flops=8 * tokens * half * width,
        moved=4 * tokens * width + 4 * half * width,
    )(plane, plane_came, out_grads)
    came = swap_square(parts, RIGHT_AWAY)
    (solved,) = call(
        cholesky_kernel, [(rank, 128)], [VMEM_SPEC] * 2, flops=rank**3, moved=8 * rank * 128
    )(plane, plane_came)
    near, far = call(
        near_far_kernel,
        [(half, owned)] * 2,
        [VMEM_SPEC] * 4 + [ANY_SPEC],
        flops=6 * half * owned,
        moved=40 * half * owned,
    )(parts[0], *came, solved)
    basis, fix = call(
        functools.partial(basis_kernel, norm_scale=norm_scale),
        [(rank, units), (rank, owned)],
        [VMEM_SPEC] * 4,
        flops=2 * rank * rank * units,
        moved=8 * rank * units,
    )(p_first, p_rest, solved, w)
    (mine,) = call(
        total_kernel,
        [(half, owned)],
        [VMEM_SPEC] * 2 + [ANY_SPEC],
        flops=half * owned,
        moved=12 * half * owned,
    )(near, swap_dp(far, SQUARE), fix)
    (factor,) = call(
        functools.partial(factor_kernel, replicas=replicas),
        [(rank, owned)],
        [VMEM_SPEC] * 4,
        [pltpu.VMEM((rank, owned), F32)],
        flops=2 * rank * rank * owned,
        moved=12 * rank * owned,
    )(mine, swap_tensor(mine, 1), solved, fix)
    return (basis.T, factor.T)


def fits(mesh, dp=8, tensor=4):
    return mesh.shape["dp"] == dp and mesh.shape["tensor"] == tensor


def solution(mesh):
    def whole(hidden, out_grad, prev_hidden, prev_grad, prev_basis, warm_start):
        norm_scale = float(prev_basis.shape[0]) ** 0.5
        body = on_device if fits(mesh) else plain_on_device
        return jax.shard_map(
            functools.partial(body, norm_scale=norm_scale),
            mesh=mesh,
            in_specs=(
                P("dp", "tensor"),
                P("dp", None),
                P("dp", "tensor"),
                P("dp", None),
                P("tensor", None),
                P(),
            ),
            out_specs=(P("tensor", None), P("dp", None)),
            check_vma=False,
        )(hidden, out_grad, prev_hidden, prev_grad, prev_basis, warm_start)

    return whole
```

```python
import functools

import jax
import jax.numpy as jnp
from jax import lax
from jax.experimental import pallas as pl
from jax.experimental.pallas import tpu as pltpu
from jax.sharding import PartitionSpec as P

F32 = jnp.float32
BF16 = jnp.bfloat16
SQUARE = 4
TERMS_AWAY = (0, 3, 2, 1)
SUMS_AWAY = (0, 3, 2, 1)
RIGHT_AWAY = (0, 3, 2, 1)
NT = (((1,), (1,)), ((), ()))
NN = (((1,), (0,)), ((), ()))
VMEM_SPEC = pl.BlockSpec(memory_space=pltpu.VMEM)
ANY_SPEC = pl.BlockSpec(memory_space=pl.ANY)
HBM_SPEC = pl.BlockSpec(memory_space=pltpu.HBM)


def orthonormal(rows_in, gram_matrix, norm_scale):
    lower = jnp.linalg.cholesky(gram_matrix)
    return norm_scale * jax.scipy.linalg.solve_triangular(lower, rows_in.T, lower=True).T


def plain_on_device(hidden, out_grad, prev_hidden, prev_grad, prev_basis, warm_start, *, norm_scale):
    highest = lax.Precision.HIGHEST
    replicas = lax.axis_size("dp")
    warm_low = warm_start.astype(BF16)
    projected = jnp.dot(out_grad, warm_low, preferred_element_type=F32).astype(BF16)
    projected_prev = jnp.dot(prev_grad, warm_low, preferred_element_type=F32).astype(BF16)
    coupling = jnp.dot(warm_start.T, warm_start, precision=highest)
    summed = jnp.einsum("tf,tr->fr", hidden, projected, preferred_element_type=F32)
    summed = summed + jnp.einsum(
        "tf,tr->fr", prev_hidden, projected_prev, preferred_element_type=F32
    )
    local_p = (summed - jnp.dot(prev_basis, coupling, precision=highest)) / replicas
    p_mean = lax.psum(local_p, "dp")
    gram_matrix = lax.psum(jnp.dot(p_mean.T, p_mean, precision=highest), "tensor")
    new_basis = orthonormal(p_mean, gram_matrix, norm_scale)
    basis_low = new_basis.astype(BF16)
    pulled = jnp.dot(hidden, basis_low, preferred_element_type=F32).astype(BF16)
    pulled_prev = jnp.dot(prev_hidden, basis_low, preferred_element_type=F32).astype(BF16)
    cross_basis = jnp.dot(prev_basis.T, new_basis, precision=highest)
    summed_q = jnp.einsum("td,tr->dr", out_grad, pulled, preferred_element_type=F32)
    summed_q = summed_q + jnp.einsum(
        "td,tr->dr", prev_grad, pulled_prev, preferred_element_type=F32
    )
    local_q = (summed_q - jnp.dot(warm_start, cross_basis, precision=highest)) / replicas
    row_count = warm_start.shape[0] // replicas
    summed_all = lax.psum(local_q, ("dp", "tensor"))
    owned_rows = lax.dynamic_slice_in_dim(
        summed_all, lax.axis_index("dp") * row_count, row_count, 0
    )
    return (new_basis, owned_rows / norm_scale)


def split(x, terms):
    parts = []
    for i in range(terms):
        part = x.astype(BF16)
        parts.append(part)
        if i + 1 < terms:
            x = x - part.astype(F32)
    return parts


def dot(a, b, dims, precision=None):
    return lax.dot_general(a, b, dims, preferred_element_type=F32, precision=precision)


def exact_dot(a, b):
    a1, a2, a3 = split(a, 3)
    b1, b2, b3 = split(b, 3)
    left = jnp.concatenate([a1, a1, a1, a2, a2, a3], axis=1)
    right = jnp.concatenate([b1, b2, b3, b1, b2, b1], axis=0)
    return dot(left, right, NN)


def chunks(extent, count):
    step = extent // count
    return [pl.ds(i * step, step) for i in range(count)]


def store_pieces(pieces, cut, summed):
    rows = pieces[0].shape[0]
    for i, piece in enumerate(pieces):
        piece[:, cut] = summed[i * rows : (i + 1) * rows]


def first_term_kernel(w_ref, o_ref, o2_ref, h_ref, h2_ref, *refs):
    pieces, (y_ref, ov, hv, wv, sem) = refs[:SQUARE], refs[SQUARE:]
    q = lax.axis_index("dp") % SQUARE
    rows = wv.shape[0] // SQUARE
    tokens = o_ref.shape[0]
    first = pieces[0].shape[1]
    copies = []

    def copy(source, target):
        copies.append(pltpu.make_async_copy(source, target, sem.at[len(copies)]))
        copies[-1].start()
        return copies[-1]

    def stacked(cut, ref, ref2, target):
        return [
            copy(r.at[:, cut], target.at[pl.ds(j * tokens, tokens), cut]) for j, r in enumerate((ref, ref2))
        ]

    def wait(pending):
        for c in pending:
            c.wait()

    o_cuts, h_cuts = chunks(o_ref.shape[1], 4), chunks(first, 2)
    w_copies = [
        copy(w_ref.at[pl.ds((q ^ m) * rows, rows), :], wv.at[pl.ds(i * rows, rows), :])
        for i, m in enumerate(TERMS_AWAY)
    ]
    o_copies = [stacked(cut, o_ref, o2_ref, ov) for cut in o_cuts]
    h_copies = [stacked(cut, h_ref, h2_ref, hv) for cut in h_cuts]
    wait(w_copies)
    projected = jnp.zeros((wv.shape[0], 2 * tokens), F32)
    for i, cut in enumerate(o_cuts):
        wait(o_copies[i])
        projected += dot(wv[:, cut].astype(BF16), ov[:, cut], NT)
    rest = stacked(pl.ds(first, h_ref.shape[1] - first), h_ref, h2_ref, hv)
    y_ref[...] = projected
    projected = projected.astype(BF16)
    for i, cut in enumerate(h_cuts):
        wait(h_copies[i])
        store_pieces(pieces, cut, dot(projected, hv[:, cut], NN))
    wait(rest)


def second_term_kernel(y_ref, h_ref, *pieces):
    first = h_ref.shape[1] - pieces[0].shape[1]
    projected = y_ref[...].astype(BF16)
    for cut, units in cuts_of(pieces, first, 2):
        store_pieces(pieces, cut, dot(projected, h_ref[:, units], NN))


def feedback_kernel(w_ref, b_ref, after_ref, first_ref, rest_ref, c_ref):
    q = lax.axis_index("dp") % SQUARE
    rank = w_ref.shape[0]
    rows = rank // SQUARE
    total = jnp.zeros((3 * rank, 3 * rank), F32)
    for cut in chunks(w_ref.shape[1], 4):
        terms = jnp.concatenate(split(w_ref[:, cut], 3), axis=0)
        total += dot(terms, terms, NT)
    total = total[:rank] + total[rank : 2 * rank] + total[2 * rank :]
    c_ref[...] = total[:, :rank] + total[:, rank : 2 * rank] + total[:, 2 * rank :]
    coupling = jnp.concatenate(
        [c_ref[pl.ds((q ^ m) * rows, rows), :] for m in SUMS_AWAY], axis=0
    )
    first = 0
    for ref in (first_ref, rest_ref):
        for cut, units in cuts_of((ref,), first, 2):
            ref[:, cut] = exact_dot(coupling, b_ref[:, units])
        first += ref.shape[1]


def pulled_rows(pieces, f_ref, h_ref, p_ref, first):
    q = lax.axis_index("dp") % SQUARE
    rows = pieces[0].shape[0]
    rank = SQUARE * rows
    pulled = jnp.zeros((2 * rank, h_ref.shape[0]), F32)
    for cut, units in cuts_of(pieces, first, 2):
        p = jnp.concatenate([s[:, cut] for s in pieces], axis=0) - f_ref[:, cut]
        for i, m in enumerate(SUMS_AWAY):
            p_ref[pl.ds((q ^ m) * rows, rows), cut] = p[i * rows : (i + 1) * rows]
        pulled += dot(jnp.concatenate(split(p, 2), axis=0), h_ref[:, units], NT)
    return pulled[:rank] + pulled[rank:]


def gram_terms(p_ref, b_ref, first):
    rank = p_ref.shape[0]
    total = jnp.zeros((3 * rank, 6 * rank), F32)
    for cut, units in cuts_of((p_ref,), first, 2):
        p = split(p_ref[:, cut], 3)
        b = split(b_ref[:, units], 3)
        total += dot(jnp.concatenate(p, axis=0), jnp.concatenate(p + b, axis=0), NT)
    total = total[:rank] + total[rank : 2 * rank] + total[2 * rank :]
    gram = total[:, :rank] + total[:, rank : 2 * rank] + total[:, 2 * rank : 3 * rank]
    cross = total[:, 3 * rank : 4 * rank] + total[:, 4 * rank : 5 * rank] + total[:, 5 * rank :]
    return jnp.concatenate([gram, cross, jnp.zeros((rank, 128 - 2 * rank), F32)], axis=1)


def cuts_of(pieces, first, count):
    cuts = chunks(pieces[0].shape[1], count)
    return [(cut, pl.ds(first + cut.start, cut.size)) for cut in cuts]


def first_pull_kernel(s0, s1, s2, s3, f_ref, h_ref, b_ref, p_ref, v_ref, g_ref):
    v_ref[...] = pulled_rows((s0, s1, s2, s3), f_ref, h_ref, p_ref, 0)
    g_ref[...] = gram_terms(p_ref, b_ref, 0)


def pull_kernel(s0, s1, s2, s3, f_ref, h_ref, v_ref, p_ref, keep_ref, send_ref, t_ref):
    q = lax.axis_index("dp") % SQUARE
    core = lax.axis_index("tensor") % 2
    rows, half = s0.shape[0], keep_ref.shape[0]
    first = h_ref.shape[1] - s0.shape[1]
    pulled = v_ref[...] + pulled_rows((s0, s1, s2, s3), f_ref, h_ref, p_ref, first)
    for i, m in enumerate(SUMS_AWAY):
        t_ref[pl.ds((q ^ m) * rows, rows), :] = pulled[i * rows : (i + 1) * rows]
    keep_ref[...] = t_ref[pl.ds(core * half, half), :]
    send_ref[...] = t_ref[pl.ds((1 - core) * half, half), :]


def gram_kernel(p_ref, b_ref, g_ref, out_ref):
    out_ref[...] = g_ref[...] + gram_terms(p_ref, b_ref, b_ref.shape[1] - p_ref.shape[1])


def push_kernel(mine_ref, got_ref, o_ref, after_ref, *outs):
    me = lax.axis_index("dp")
    tokens = o_ref.shape[0]
    half, width = outs[0].shape[1:]
    v = jnp.concatenate(split(mine_ref[...] + got_ref[...], 2), axis=0)
    for i, m in enumerate(RIGHT_AWAY):
        for z in range(2):
            cut = pl.ds(pl.multiple_of((me ^ m ^ (SQUARE * z)) * width, width), width)
            both = dot(v, o_ref[:, cut], NN)
            outs[i][z] = both[:half] + both[half:]


def cholesky_kernel(mine_ref, got_ref, out_ref):
    rank = out_ref.shape[0]
    shape, block = out_ref.shape, 8
    row = lax.broadcasted_iota(jnp.int32, shape, 0)
    lane = lax.broadcasted_iota(jnp.int32, shape, 1)
    a = jnp.where(lane == row + 2 * rank, 1.0, mine_ref[...] + got_ref[...])
    for k in range(0, rank, block):
        rows = [jnp.broadcast_to(a[k + i : k + i + 1, :], shape) for i in range(block)]
        columns = [jnp.broadcast_to(a[:, k + i : k + i + 1], shape) for i in range(block)]
        change = jnp.zeros(shape, F32)
        for i in range(block):
            inverse = 1.0 / columns[i][k + i : k + i + 1, :]
            change += jnp.where(row > k + i, columns[i], 0.0) * (rows[i] * inverse)
            for j in range(i + 1, block):
                factor = columns[i][k + j : k + j + 1, :] * inverse
                rows[j] = rows[j] - factor * rows[i]
                columns[j] = columns[j] - factor * columns[i]
        a = a - change
    pivots = jnp.sum(jnp.where(lane == row, a, 0.0), axis=1, keepdims=True)
    out_ref[...] = a * (1.0 / jnp.sqrt(pivots))


def near_far_kernel(a_ref, b_ref, c_ref, d_ref, after_ref, near_ref, far_ref):
    near_ref[...] = a_ref[0] + b_ref[0] + c_ref[0] + d_ref[0]
    far_ref[...] = a_ref[1] + b_ref[1] + c_ref[1] + d_ref[1]


def total_kernel(a_ref, b_ref, after_ref, out_ref):
    out_ref[...] = a_ref[...] + b_ref[...]


def basis_kernel(p_ref, r_ref, l_ref, w_ref, out_ref, fix_ref, *, norm_scale):
    rank = l_ref.shape[0]
    width = fix_ref.shape[1]
    inverse = l_ref[:, 2 * rank : 3 * rank] * norm_scale
    first = 0
    for ref in (p_ref, r_ref):
        for cut, units in cuts_of((ref,), first, 2):
            out_ref[:, units] = exact_dot(inverse, ref[:, cut])
        first += ref.shape[1]
    own = pl.ds(pl.multiple_of(lax.axis_index("dp") * width, width), width)
    fix_ref[...] = exact_dot(l_ref[:, rank : 2 * rank], w_ref[:, own])


def factor_kernel(t_ref, u_ref, l_ref, fix_ref, out_ref, z_ref, *, replicas):
    core = lax.axis_index("tensor") % 2
    half = t_ref.shape[0]
    rank = 2 * half
    z_ref[pl.ds(core * half, half), :] = t_ref[...]
    z_ref[pl.ds((1 - core) * half, half), :] = u_ref[...]
    inverse = l_ref[:, 2 * rank : 3 * rank] * (1.0 / replicas)
    out_ref[...] = exact_dot(inverse, z_ref[...]) - fix_ref[...]


def call(kernel, outs, specs, scratch=(), flops=0, moved=0, vmem=32 << 20):
    return pl.pallas_call(
        kernel,
        out_shape=[jax.ShapeDtypeStruct(shape[:2] if BF16 in shape else shape, BF16 if BF16 in shape else F32) for shape in outs],
        in_specs=specs,
        out_specs=[VMEM_SPEC] * len(outs),
        scratch_shapes=scratch,
        compiler_params=pltpu.CompilerParams(vmem_limit_bytes=vmem),
        cost_estimate=pl.CostEstimate(flops=flops, bytes_accessed=moved, transcendentals=0),
    )


def in_hbm(x):
    return pltpu.with_memory_space_constraint(x, pltpu.HBM)


def swap_dp(x, m):
    n = lax.axis_size("dp")
    return lax.ppermute(x, "dp", [(i, i ^ m) for i in range(n)])


def swap_tensor(x, m):
    n = lax.axis_size("tensor")
    return lax.ppermute(x, "tensor", [(i, i ^ m) for i in range(n)])


def on_device(hidden, out_grad, prev_hidden, prev_grad, prev_basis, warm_start, *, norm_scale):
    replicas = lax.axis_size("dp")
    tokens, units = hidden.shape
    width = out_grad.shape[1]
    rank = warm_start.shape[1]
    rows, half, owned = rank // SQUARE, rank // 2, width // replicas
    w, b = warm_start.T, prev_basis.T
    first = units // 256 * 128
    rest = units - first

    *terms, projected, out_grads, hiddens = call(
        first_term_kernel,
        [(rows, first)] * SQUARE + [(rank, 2 * tokens), (2 * tokens, width, BF16), (2 * tokens, units, BF16)],
        [HBM_SPEC] * 5,
        [pltpu.VMEM((rank, width), F32), pltpu.SemaphoreType.DMA((18,))],
        flops=4 * tokens * rank * (first + width),
        moved=4 * tokens * (units + width) + 4 * rank * (first + width),
    )(*[in_hbm(x) for x in (w, out_grad, prev_grad, hidden, prev_hidden)])
    late_terms = call(
        second_term_kernel,
        [(rows, rest)] * SQUARE,
        [VMEM_SPEC] * 2,
        flops=4 * tokens * rank * rest,
        moved=4 * tokens * rest + 4 * rank * rest,
    )(projected, hiddens)

    def swap_square(x, away):
        return [swap_dp(x[i], m) for i, m in enumerate(away) if m]

    def mean(summed, came):
        own = (summed + came) * (1.0 / replicas)
        return [own] + swap_square([own] * SQUARE, SUMS_AWAY)

    early = terms[0] + sum(swap_square(terms, TERMS_AWAY))
    early_came = swap_dp(early, SQUARE)
    late = late_terms[0] + sum(swap_square(late_terms, TERMS_AWAY))
    late_came = swap_dp(late, SQUARE)
    early_feedback, late_feedback = call(
        feedback_kernel,
        [(rank, first), (rank, rest)],
        [VMEM_SPEC] * 2 + [ANY_SPEC],
        [pltpu.VMEM((rank, rank), F32)],
        flops=2 * rank * rank * (units + width),
        moved=4 * rank * (units + width),
    )(w, b, late)
    early_came, early_feedback = lax.optimization_barrier((early_came, early_feedback))
    early_p = mean(early, early_came)
    late_p = mean(late, late_came)

    p_first, early_v, early_gram = call(
        first_pull_kernel,
        [(rank, first), (rank, 2 * tokens), (rank, 128)],
        [VMEM_SPEC] * 7,
        flops=8 * tokens * rank * first,
        moved=4 * tokens * first + 4 * rank * first,
    )(*early_p, early_feedback, hiddens, b)
    p_rest, keep, send = call(
        pull_kernel,
        [(rank, rest)] + [(half, 2 * tokens)] * 2,
        [VMEM_SPEC] * 7,
        [pltpu.VMEM((rank, 2 * tokens), F32)],
        flops=8 * tokens * rank * rest,
        moved=4 * tokens * rest + 4 * rank * rest,
    )(*late_p, late_feedback, hiddens, early_v)
    other = swap_tensor(send, 1)
    (gram,) = call(
        gram_kernel,
        [(rank, 128)],
        [VMEM_SPEC] * 3,
        flops=36 * rank * rank * rest,
        moved=8 * rank * rest,
    )(p_rest, b, early_gram)
    other, gram = lax.optimization_barrier((other, gram))
    plane = keep + other
    plane_came = swap_tensor(plane, 2)
    gram = gram + swap_tensor(gram, 1)
    gram_came = swap_tensor(gram, 2)
    parts = call(
        push_kernel,
        [(2, half, owned)] * SQUARE,
        [VMEM_SPEC] * 3 + [ANY_SPEC],
        flops=8 * tokens * half * width,
        moved=4 * tokens * width + 4 * half * width,
    )(plane, plane_came, out_grads, gram)
    came = swap_square(parts, RIGHT_AWAY)
    (solved,) = call(
        cholesky_kernel, [(rank, 128)], [VMEM_SPEC] * 2, flops=rank**3, moved=8 * rank * 128
    )(gram, gram_came)
    near, far = call(
        near_far_kernel,
        [(half, owned)] * 2,
        [VMEM_SPEC] * 4 + [ANY_SPEC],
        flops=6 * half * owned,
        moved=40 * half * owned,
    )(parts[0], *came, solved)
    basis, fix = call(
        functools.partial(basis_kernel, norm_scale=norm_scale),
        [(rank, units), (rank, owned)],
        [VMEM_SPEC] * 4,
        flops=2 * rank * rank * units,
        moved=8 * rank * units,
    )(p_first, p_rest, solved, w)
    (mine,) = call(
        total_kernel,
        [(half, owned)],
        [VMEM_SPEC] * 2 + [ANY_SPEC],
        flops=half * owned,
        moved=12 * half * owned,
    )(near, swap_dp(far, SQUARE), fix)
    (factor,) = call(
        functools.partial(factor_kernel, replicas=replicas),
        [(rank, owned)],
        [VMEM_SPEC] * 4,
        [pltpu.VMEM((rank, owned), F32)],
        flops=2 * rank * rank * owned,
        moved=12 * rank * owned,
    )(mine, swap_tensor(mine, 1), solved, fix)
    return (basis.T, factor.T)


def fits(mesh, dp=8, tensor=4):
    return mesh.shape["dp"] == dp and mesh.shape["tensor"] == tensor


def solution(mesh):
    def whole(hidden, out_grad, prev_hidden, prev_grad, prev_basis, warm_start):
        norm_scale = float(prev_basis.shape[0]) ** 0.5
        body = on_device if fits(mesh) else plain_on_device
        return jax.shard_map(
            functools.partial(body, norm_scale=norm_scale),
            mesh=mesh,
            in_specs=(
                P("dp", "tensor"),
                P("dp", None),
                P("dp", "tensor"),
                P("dp", None),
                P("tensor", None),
                P(),
            ),
            out_specs=(P("tensor", None), P("dp", None)),
            check_vma=False,
        )(hidden, out_grad, prev_hidden, prev_grad, prev_basis, warm_start)

    return whole
```

```python
import functools

import jax
import jax.numpy as jnp
from jax import lax
from jax.experimental import pallas as pl
from jax.experimental.pallas import tpu as pltpu
from jax.sharding import PartitionSpec as P

F32 = jnp.float32
BF16 = jnp.bfloat16
SQUARE = 4
TERMS_AWAY = (0, 3, 2, 1)
SUMS_AWAY = (0, 3, 2, 1)
RIGHT_AWAY = (0, 3, 2, 1)
NT = (((1,), (1,)), ((), ()))
NN = (((1,), (0,)), ((), ()))
VMEM_SPEC = pl.BlockSpec(memory_space=pltpu.VMEM)
ANY_SPEC = pl.BlockSpec(memory_space=pl.ANY)
HBM_SPEC = pl.BlockSpec(memory_space=pltpu.HBM)


def orthonormal(rows_in, gram_matrix, norm_scale):
    lower = jnp.linalg.cholesky(gram_matrix)
    return norm_scale * jax.scipy.linalg.solve_triangular(lower, rows_in.T, lower=True).T


def plain_on_device(hidden, out_grad, prev_hidden, prev_grad, prev_basis, warm_start, *, norm_scale):
    highest = lax.Precision.HIGHEST
    replicas = lax.axis_size("dp")
    warm_low = warm_start.astype(BF16)
    projected = jnp.dot(out_grad, warm_low, preferred_element_type=F32).astype(BF16)
    projected_prev = jnp.dot(prev_grad, warm_low, preferred_element_type=F32).astype(BF16)
    coupling = jnp.dot(warm_start.T, warm_start, precision=highest)
    summed = jnp.einsum("tf,tr->fr", hidden, projected, preferred_element_type=F32)
    summed = summed + jnp.einsum(
        "tf,tr->fr", prev_hidden, projected_prev, preferred_element_type=F32
    )
    local_p = (summed - jnp.dot(prev_basis, coupling, precision=highest)) / replicas
    p_mean = lax.psum(local_p, "dp")
    gram_matrix = lax.psum(jnp.dot(p_mean.T, p_mean, precision=highest), "tensor")
    new_basis = orthonormal(p_mean, gram_matrix, norm_scale)
    basis_low = new_basis.astype(BF16)
    pulled = jnp.dot(hidden, basis_low, preferred_element_type=F32).astype(BF16)
    pulled_prev = jnp.dot(prev_hidden, basis_low, preferred_element_type=F32).astype(BF16)
    cross_basis = jnp.dot(prev_basis.T, new_basis, precision=highest)
    summed_q = jnp.einsum("td,tr->dr", out_grad, pulled, preferred_element_type=F32)
    summed_q = summed_q + jnp.einsum(
        "td,tr->dr", prev_grad, pulled_prev, preferred_element_type=F32
    )
    local_q = (summed_q - jnp.dot(warm_start, cross_basis, precision=highest)) / replicas
    row_count = warm_start.shape[0] // replicas
    summed_all = lax.psum(local_q, ("dp", "tensor"))
    owned_rows = lax.dynamic_slice_in_dim(
        summed_all, lax.axis_index("dp") * row_count, row_count, 0
    )
    return (new_basis, owned_rows / norm_scale)


def split(x, terms):
    parts = []
    for i in range(terms):
        part = x.astype(BF16)
        parts.append(part)
        if i + 1 < terms:
            x = x - part.astype(F32)
    return parts


def dot(a, b, dims, precision=None):
    return lax.dot_general(a, b, dims, preferred_element_type=F32, precision=precision)


def exact_dot(a, b):
    a1, a2, a3 = split(a, 3)
    b1, b2, b3 = split(b, 3)
    left = jnp.concatenate([a1, a1, a1, a2, a2, a3], axis=1)
    right = jnp.concatenate([b1, b2, b3, b1, b2, b1], axis=0)
    return dot(left, right, NN)


def chunks(extent, count):
    step = extent // count
    return [pl.ds(i * step, step) for i in range(count)]


def store_pieces(pieces, cut, summed):
    rows = pieces[0].shape[0]
    for i, piece in enumerate(pieces):
        piece[:, cut] = summed[i * rows : (i + 1) * rows]


def first_term_kernel(w_ref, o_ref, o2_ref, h_ref, h2_ref, *refs):
    pieces, (y_ref, ov, hv, wv, sem) = refs[:SQUARE], refs[SQUARE:]
    q = lax.axis_index("dp") % SQUARE
    rows = wv.shape[0] // SQUARE
    tokens = o_ref.shape[0]
    first = pieces[0].shape[1]
    copies = []

    def copy(source, target):
        copies.append(pltpu.make_async_copy(source, target, sem.at[len(copies)]))
        copies[-1].start()
        return copies[-1]

    def stacked(cut, ref, ref2, target):
        return [
            copy(r.at[:, cut], target.at[pl.ds(j * tokens, tokens), cut]) for j, r in enumerate((ref, ref2))
        ]

    def wait(pending):
        for c in pending:
            c.wait()

    o_cuts, h_cuts = chunks(o_ref.shape[1], 4), chunks(first, 2)
    w_copies = [
        copy(w_ref.at[pl.ds((q ^ m) * rows, rows), :], wv.at[pl.ds(i * rows, rows), :])
        for i, m in enumerate(TERMS_AWAY)
    ]
    o_copies = [stacked(cut, o_ref, o2_ref, ov) for cut in o_cuts]
    h_copies = [stacked(cut, h_ref, h2_ref, hv) for cut in h_cuts]
    wait(w_copies)
    projected = jnp.zeros((wv.shape[0], 2 * tokens), F32)
    for i, cut in enumerate(o_cuts):
        wait(o_copies[i])
        projected += dot(wv[:, cut].astype(BF16), ov[:, cut], NT)
    rest = stacked(pl.ds(first, h_ref.shape[1] - first), h_ref, h2_ref, hv)
    y_ref[...] = projected
    projected = projected.astype(BF16)
    for i, cut in enumerate(h_cuts):
        wait(h_copies[i])
        store_pieces(pieces, cut, dot(projected, hv[:, cut], NN))
    wait(rest)


def second_term_kernel(y_ref, h_ref, *pieces):
    first = h_ref.shape[1] - pieces[0].shape[1]
    projected = y_ref[...].astype(BF16)
    for cut, units in cuts_of(pieces, first, 2):
        store_pieces(pieces, cut, dot(projected, h_ref[:, units], NN))


def feedback_kernel(w_ref, b_ref, after_ref, first_ref, rest_ref, c_ref):
    q = lax.axis_index("dp") % SQUARE
    rank = w_ref.shape[0]
    rows = rank // SQUARE
    total = jnp.zeros((3 * rank, 3 * rank), F32)
    for cut in chunks(w_ref.shape[1], 4):
        terms = jnp.concatenate(split(w_ref[:, cut], 3), axis=0)
        total += dot(terms, terms, NT)
    total = total[:rank] + total[rank : 2 * rank] + total[2 * rank :]
    c_ref[...] = total[:, :rank] + total[:, rank : 2 * rank] + total[:, 2 * rank :]
    coupling = jnp.concatenate(
        [c_ref[pl.ds((q ^ m) * rows, rows), :] for m in SUMS_AWAY], axis=0
    )
    first = 0
    for ref in (first_ref, rest_ref):
        for cut, units in cuts_of((ref,), first, 2):
            ref[:, cut] = exact_dot(coupling, b_ref[:, units])
        first += ref.shape[1]


def pulled_rows(pieces, f_ref, h_ref, p_ref, first):
    q = lax.axis_index("dp") % SQUARE
    rows = pieces[0].shape[0]
    rank = SQUARE * rows
    pulled = jnp.zeros((2 * rank, h_ref.shape[0]), F32)
    for cut, units in cuts_of(pieces, first, 2):
        p = jnp.concatenate([s[:, cut] for s in pieces], axis=0) - f_ref[:, cut]
        for i, m in enumerate(SUMS_AWAY):
            p_ref[pl.ds((q ^ m) * rows, rows), cut] = p[i * rows : (i + 1) * rows]
        pulled += dot(jnp.concatenate(split(p, 2), axis=0), h_ref[:, units], NT)
    return pulled[:rank] + pulled[rank:]


def gram_terms(p_ref, b_ref, first):
    rank = p_ref.shape[0]
    total = jnp.zeros((3 * rank, 6 * rank), F32)
    for cut, units in cuts_of((p_ref,), first, 2):
        p = split(p_ref[:, cut], 3)
        b = split(b_ref[:, units], 3)
        total += dot(jnp.concatenate(p, axis=0), jnp.concatenate(p + b, axis=0), NT)
    total = total[:rank] + total[rank : 2 * rank] + total[2 * rank :]
    gram = total[:, :rank] + total[:, rank : 2 * rank] + total[:, 2 * rank : 3 * rank]
    cross = total[:, 3 * rank : 4 * rank] + total[:, 4 * rank : 5 * rank] + total[:, 5 * rank :]
    return jnp.concatenate([gram, cross, jnp.zeros((rank, 128 - 2 * rank), F32)], axis=1)


def cuts_of(pieces, first, count):
    cuts = chunks(pieces[0].shape[1], count)
    return [(cut, pl.ds(first + cut.start, cut.size)) for cut in cuts]


def first_pull_kernel(s0, s1, s2, s3, f_ref, h_ref, b_ref, p_ref, v_ref, g_ref):
    v_ref[...] = pulled_rows((s0, s1, s2, s3), f_ref, h_ref, p_ref, 0)
    g_ref[...] = gram_terms(p_ref, b_ref, 0)


def side():
    tensor = lax.axis_index("tensor")
    return (tensor ^ (tensor // 2)) % 2


def pull_kernel(s0, s1, s2, s3, f_ref, h_ref, v_ref, p_ref, keep_ref, send_ref, t_ref):
    q = lax.axis_index("dp") % SQUARE
    mine = side()
    rows, half = s0.shape[0], keep_ref.shape[0]
    first = h_ref.shape[1] - s0.shape[1]
    pulled = v_ref[...] + pulled_rows((s0, s1, s2, s3), f_ref, h_ref, p_ref, first)
    for i, m in enumerate(SUMS_AWAY):
        t_ref[pl.ds((q ^ m) * rows, rows), :] = pulled[i * rows : (i + 1) * rows]
    keep_ref[...] = t_ref[pl.ds(mine * half, half), :]
    send_ref[...] = t_ref[pl.ds((1 - mine) * half, half), :]


def gram_kernel(p_ref, b_ref, g_ref, keep_ref, out_ref):
    grams = g_ref[...] + gram_terms(p_ref, b_ref, b_ref.shape[1] - p_ref.shape[1])
    half, tokens = keep_ref.shape
    out_ref[:, :tokens] = keep_ref[...]
    out_ref[:, tokens : tokens + 128] = grams[:half]
    out_ref[:, tokens + 128 :] = grams[half:]


def push_kernel(mine_ref, got_ref, o_ref, *outs):
    me = lax.axis_index("dp")
    up = lax.axis_index("tensor") // 2
    tokens = o_ref.shape[0]
    half, width = outs[0].shape[1:]
    v = jnp.concatenate(split(mine_ref[:, :tokens] + got_ref[:, :tokens], 2), axis=0)
    for i, m in enumerate(RIGHT_AWAY):
        for z in range(2):
            start = pl.multiple_of((me ^ m ^ (SQUARE * z)) * (2 * width) + up * width, width)
            both = dot(v, o_ref[:, pl.ds(start, width)], NN)
            outs[i][z] = both[:half] + both[half:]


def cholesky_kernel(mine_ref, got_ref, out_ref):
    rank = out_ref.shape[0]
    shape, block = out_ref.shape, 8
    row = lax.broadcasted_iota(jnp.int32, shape, 0)
    lane = lax.broadcasted_iota(jnp.int32, shape, 1)
    grams = mine_ref[...] + got_ref[...]
    grams = jnp.concatenate([grams[:, : shape[1]], grams[:, shape[1] :]], axis=0)
    a = jnp.where(lane == row + 2 * rank, 1.0, grams)
    for k in range(0, rank, block):
        rows = [jnp.broadcast_to(a[k + i : k + i + 1, :], shape) for i in range(block)]
        columns = [jnp.broadcast_to(a[:, k + i : k + i + 1], shape) for i in range(block)]
        change = jnp.zeros(shape, F32)
        for i in range(block):
            inverse = 1.0 / columns[i][k + i : k + i + 1, :]
            change += jnp.where(row > k + i, columns[i], 0.0) * (rows[i] * inverse)
            for j in range(i + 1, block):
                factor = columns[i][k + j : k + j + 1, :] * inverse
                rows[j] = rows[j] - factor * rows[i]
                columns[j] = columns[j] - factor * columns[i]
        a = a - change
    pivots = jnp.sum(jnp.where(lane == row, a, 0.0), axis=1, keepdims=True)
    out_ref[...] = a * (1.0 / jnp.sqrt(pivots))


def near_far_kernel(a_ref, b_ref, c_ref, d_ref, after_ref, near_ref, far_ref):
    near_ref[...] = a_ref[0] + b_ref[0] + c_ref[0] + d_ref[0]
    far_ref[...] = a_ref[1] + b_ref[1] + c_ref[1] + d_ref[1]


def total_kernel(up_far_ref, far_ref, up_near_ref, near_ref, after_ref, out_ref):
    up = lax.axis_index("tensor") // 2
    width = near_ref.shape[1]
    mine = pl.ds(pl.multiple_of(up * width, width), width)
    other = pl.ds(pl.multiple_of((1 - up) * width, width), width)
    out_ref[:, mine] = near_ref[...] + far_ref[...]
    out_ref[:, other] = up_near_ref[...] + up_far_ref[...]


def basis_kernel(p_ref, r_ref, l_ref, w_ref, out_ref, fix_ref, *, norm_scale):
    rank = l_ref.shape[0]
    width = fix_ref.shape[1]
    inverse = l_ref[:, 2 * rank : 3 * rank] * norm_scale
    first = 0
    for ref in (p_ref, r_ref):
        for cut, units in cuts_of((ref,), first, 2):
            out_ref[:, units] = exact_dot(inverse, ref[:, cut])
        first += ref.shape[1]
    own = pl.ds(pl.multiple_of(lax.axis_index("dp") * width, width), width)
    fix_ref[...] = exact_dot(l_ref[:, rank : 2 * rank], w_ref[:, own])


def factor_kernel(t_ref, u_ref, l_ref, fix_ref, out_ref, z_ref, *, replicas):
    mine = side()
    half = t_ref.shape[0]
    rank = 2 * half
    z_ref[pl.ds(mine * half, half), :] = t_ref[...]
    z_ref[pl.ds((1 - mine) * half, half), :] = u_ref[...]
    inverse = l_ref[:, 2 * rank : 3 * rank] * (1.0 / replicas)
    out_ref[...] = exact_dot(inverse, z_ref[...]) - fix_ref[...]


def call(kernel, outs, specs, scratch=(), flops=0, moved=0, vmem=32 << 20):
    return pl.pallas_call(
        kernel,
        out_shape=[jax.ShapeDtypeStruct(shape[:2] if BF16 in shape else shape, BF16 if BF16 in shape else F32) for shape in outs],
        in_specs=specs,
        out_specs=[VMEM_SPEC] * len(outs),
        scratch_shapes=scratch,
        compiler_params=pltpu.CompilerParams(vmem_limit_bytes=vmem),
        cost_estimate=pl.CostEstimate(flops=flops, bytes_accessed=moved, transcendentals=0),
    )


def in_hbm(x):
    return pltpu.with_memory_space_constraint(x, pltpu.HBM)


def swap_dp(x, m):
    n = lax.axis_size("dp")
    return lax.ppermute(x, "dp", [(i, i ^ m) for i in range(n)])


def swap_tensor(x, m):
    n = lax.axis_size("tensor")
    return lax.ppermute(x, "tensor", [(i, i ^ m) for i in range(n)])


def swap_both(x, md, mt):
    n, k = lax.axis_size("dp"), lax.axis_size("tensor")
    pairs = [(i * k + t, (i ^ md) * k + (t ^ mt)) for i in range(n) for t in range(k)]
    return lax.ppermute(x, ("dp", "tensor"), pairs)


def on_device(hidden, out_grad, prev_hidden, prev_grad, prev_basis, warm_start, *, norm_scale):
    replicas = lax.axis_size("dp")
    tokens, units = hidden.shape
    width = out_grad.shape[1]
    rank = warm_start.shape[1]
    rows, half, owned = rank // SQUARE, rank // 2, width // replicas
    w, b = warm_start.T, prev_basis.T
    first = units // 256 * 128
    rest = units - first

    *terms, projected, out_grads, hiddens = call(
        first_term_kernel,
        [(rows, first)] * SQUARE + [(rank, 2 * tokens), (2 * tokens, width, BF16), (2 * tokens, units, BF16)],
        [HBM_SPEC] * 5,
        [pltpu.VMEM((rank, width), F32), pltpu.SemaphoreType.DMA((18,))],
        flops=4 * tokens * rank * (first + width),
        moved=4 * tokens * (units + width) + 4 * rank * (first + width),
    )(*[in_hbm(x) for x in (w, out_grad, prev_grad, hidden, prev_hidden)])
    late_terms = call(
        second_term_kernel,
        [(rows, rest)] * SQUARE,
        [VMEM_SPEC] * 2,
        flops=4 * tokens * rank * rest,
        moved=4 * tokens * rest + 4 * rank * rest,
    )(projected, hiddens)

    def swap_square(x, away):
        return [swap_dp(x[i], m) for i, m in enumerate(away) if m]

    def mean(summed, came):
        own = (summed + came) * (1.0 / replicas)
        return [own] + swap_square([own] * SQUARE, SUMS_AWAY)

    early = terms[0] + sum(swap_square(terms, TERMS_AWAY))
    early_came = swap_dp(early, SQUARE)
    late = late_terms[0] + sum(swap_square(late_terms, TERMS_AWAY))
    late_came = swap_dp(late, SQUARE)
    early_feedback, late_feedback = call(
        feedback_kernel,
        [(rank, first), (rank, rest)],
        [VMEM_SPEC] * 2 + [ANY_SPEC],
        [pltpu.VMEM((rank, rank), F32)],
        flops=2 * rank * rank * (units + width),
        moved=4 * rank * (units + width),
    )(w, b, late)
    early_came, early_feedback = lax.optimization_barrier((early_came, early_feedback))
    early_p = mean(early, early_came)
    late_p = mean(late, late_came)

    p_first, early_v, early_gram = call(
        first_pull_kernel,
        [(rank, first), (rank, 2 * tokens), (rank, 128)],
        [VMEM_SPEC] * 7,
        flops=8 * tokens * rank * first,
        moved=4 * tokens * first + 4 * rank * first,
    )(*early_p, early_feedback, hiddens, b)
    p_rest, keep, send = call(
        pull_kernel,
        [(rank, rest)] + [(half, 2 * tokens)] * 2,
        [VMEM_SPEC] * 7,
        [pltpu.VMEM((rank, 2 * tokens), F32)],
        flops=8 * tokens * rank * rest,
        moved=4 * tokens * rest + 4 * rank * rest,
    )(*late_p, late_feedback, hiddens, early_v)
    other = swap_tensor(send, 1)
    (kept,) = call(
        gram_kernel,
        [(half, 2 * tokens + 256)],
        [VMEM_SPEC] * 4,
        flops=36 * rank * rank * rest,
        moved=8 * rank * rest,
    )(p_rest, b, early_gram, keep)
    plane = kept + jnp.pad(other, ((0, 0), (0, 256)))
    plane_came = swap_both(plane, 0, 3)
    grams = (plane + plane_came)[:, 2 * tokens :]
    grams_came = swap_tensor(grams, 1)
    parts = call(
        push_kernel,
        [(2, half, owned // 2)] * SQUARE,
        [VMEM_SPEC] * 3,
        flops=8 * tokens * half * width,
        moved=4 * tokens * width + 4 * half * width,
    )(plane, plane_came, out_grads)
    came = swap_square(parts, RIGHT_AWAY)
    (solved,) = call(
        cholesky_kernel, [(rank, 128)], [VMEM_SPEC] * 2, flops=rank**3, moved=8 * rank * 128
    )(grams, grams_came)
    near, far = call(
        near_far_kernel,
        [(half, owned // 2)] * 2,
        [VMEM_SPEC] * 4 + [ANY_SPEC],
        flops=6 * half * owned,
        moved=40 * half * owned,
    )(parts[0], *came, solved)
    basis, fix = call(
        functools.partial(basis_kernel, norm_scale=norm_scale),
        [(rank, units), (rank, owned)],
        [VMEM_SPEC] * 4,
        flops=2 * rank * rank * units,
        moved=8 * rank * units,
    )(p_first, p_rest, solved, w)
    up_far = swap_both(far, SQUARE, 3)
    far_came = swap_both(far, SQUARE, 0)
    up_near = swap_both(near, 0, 3)
    (mine,) = call(
        total_kernel,
        [(half, owned)],
        [VMEM_SPEC] * 4 + [ANY_SPEC],
        flops=half * owned,
        moved=12 * half * owned,
    )(up_far, far_came, up_near, near, fix)
    (factor,) = call(
        functools.partial(factor_kernel, replicas=replicas),
        [(rank, owned)],
        [VMEM_SPEC] * 4,
        [pltpu.VMEM((rank, owned), F32)],
        flops=2 * rank * rank * owned,
        moved=12 * rank * owned,
    )(mine, swap_tensor(mine, 1), solved, fix)
    return (basis.T, factor.T)


def fits(mesh, dp=8, tensor=4):
    return mesh.shape["dp"] == dp and mesh.shape["tensor"] == tensor


def solution(mesh):
    def whole(hidden, out_grad, prev_hidden, prev_grad, prev_basis, warm_start):
        norm_scale = float(prev_basis.shape[0]) ** 0.5
        body = on_device if fits(mesh) else plain_on_device
        return jax.shard_map(
            functools.partial(body, norm_scale=norm_scale),
            mesh=mesh,
            in_specs=(
                P("dp", "tensor"),
                P("dp", None),
                P("dp", "tensor"),
                P("dp", None),
                P("tensor", None),
                P(),
            ),
            out_specs=(P("tensor", None), P("dp", None)),
            check_vma=False,
        )(hidden, out_grad, prev_hidden, prev_grad, prev_basis, warm_start)

    return whole
```

```python
import functools

import jax
import jax.numpy as jnp
from jax import lax
from jax.experimental import pallas as pl
from jax.experimental.pallas import tpu as pltpu
from jax.sharding import PartitionSpec as P

F32 = jnp.float32
BF16 = jnp.bfloat16
SQUARE = 4
TERMS_AWAY = (0, 3, 2, 1)
SUMS_AWAY = (0, 3, 2, 1)
RIGHT_AWAY = (0, 3, 2, 1)
NT = (((1,), (1,)), ((), ()))
NN = (((1,), (0,)), ((), ()))
VMEM_SPEC = pl.BlockSpec(memory_space=pltpu.VMEM)
ANY_SPEC = pl.BlockSpec(memory_space=pl.ANY)
HBM_SPEC = pl.BlockSpec(memory_space=pltpu.HBM)


def orthonormal(rows_in, gram_matrix, norm_scale):
    lower = jnp.linalg.cholesky(gram_matrix)
    return norm_scale * jax.scipy.linalg.solve_triangular(lower, rows_in.T, lower=True).T


def plain_on_device(hidden, out_grad, prev_hidden, prev_grad, prev_basis, warm_start, *, norm_scale):
    highest = lax.Precision.HIGHEST
    replicas = lax.axis_size("dp")
    warm_low = warm_start.astype(BF16)
    projected = jnp.dot(out_grad, warm_low, preferred_element_type=F32).astype(BF16)
    projected_prev = jnp.dot(prev_grad, warm_low, preferred_element_type=F32).astype(BF16)
    coupling = jnp.dot(warm_start.T, warm_start, precision=highest)
    summed = jnp.einsum("tf,tr->fr", hidden, projected, preferred_element_type=F32)
    summed = summed + jnp.einsum(
        "tf,tr->fr", prev_hidden, projected_prev, preferred_element_type=F32
    )
    local_p = (summed - jnp.dot(prev_basis, coupling, precision=highest)) / replicas
    p_mean = lax.psum(local_p, "dp")
    gram_matrix = lax.psum(jnp.dot(p_mean.T, p_mean, precision=highest), "tensor")
    new_basis = orthonormal(p_mean, gram_matrix, norm_scale)
    basis_low = new_basis.astype(BF16)
    pulled = jnp.dot(hidden, basis_low, preferred_element_type=F32).astype(BF16)
    pulled_prev = jnp.dot(prev_hidden, basis_low, preferred_element_type=F32).astype(BF16)
    cross_basis = jnp.dot(prev_basis.T, new_basis, precision=highest)
    summed_q = jnp.einsum("td,tr->dr", out_grad, pulled, preferred_element_type=F32)
    summed_q = summed_q + jnp.einsum(
        "td,tr->dr", prev_grad, pulled_prev, preferred_element_type=F32
    )
    local_q = (summed_q - jnp.dot(warm_start, cross_basis, precision=highest)) / replicas
    row_count = warm_start.shape[0] // replicas
    summed_all = lax.psum(local_q, ("dp", "tensor"))
    owned_rows = lax.dynamic_slice_in_dim(
        summed_all, lax.axis_index("dp") * row_count, row_count, 0
    )
    return (new_basis, owned_rows / norm_scale)


def split(x, terms):
    parts = []
    for i in range(terms):
        part = x.astype(BF16)
        parts.append(part)
        if i + 1 < terms:
            x = x - part.astype(F32)
    return parts


def dot(a, b, dims, precision=None):
    return lax.dot_general(a, b, dims, preferred_element_type=F32, precision=precision)


def exact_dot(a, b):
    a1, a2, a3 = split(a, 3)
    b1, b2, b3 = split(b, 3)
    left = jnp.concatenate([a1, a1, a1, a2, a2, a3], axis=1)
    right = jnp.concatenate([b1, b2, b3, b1, b2, b1], axis=0)
    return dot(left, right, NN)


def chunks(extent, count):
    step = extent // count
    return [pl.ds(i * step, step) for i in range(count)]


def store_pieces(pieces, cut, summed):
    rows = pieces[0].shape[0]
    for i, piece in enumerate(pieces):
        piece[:, cut] = summed[i * rows : (i + 1) * rows]


def first_term_kernel(w_ref, o_ref, o2_ref, h_ref, h2_ref, *refs):
    pieces, (y_ref, ov, hv, wv, sem) = refs[:SQUARE], refs[SQUARE:]
    q = lax.axis_index("dp") % SQUARE
    rows = wv.shape[0] // SQUARE
    tokens = o_ref.shape[0]
    first = pieces[0].shape[1]
    copies = []

    def copy(source, target):
        copies.append(pltpu.make_async_copy(source, target, sem.at[len(copies)]))
        copies[-1].start()
        return copies[-1]

    def stacked(cut, ref, ref2, target):
        return [
            copy(r.at[:, cut], target.at[pl.ds(j * tokens, tokens), cut]) for j, r in enumerate((ref, ref2))
        ]

    def wait(pending):
        for c in pending:
            c.wait()

    o_cuts, h_cuts = chunks(o_ref.shape[1], 4), chunks(first, 2)
    w_copies = [
        copy(w_ref.at[pl.ds((q ^ m) * rows, rows), :], wv.at[pl.ds(i * rows, rows), :])
        for i, m in enumerate(TERMS_AWAY)
    ]
    o_copies = [stacked(cut, o_ref, o2_ref, ov) for cut in o_cuts]
    h_copies = [stacked(cut, h_ref, h2_ref, hv) for cut in h_cuts]
    wait(w_copies)
    projected = jnp.zeros((wv.shape[0], 2 * tokens), F32)
    for i, cut in enumerate(o_cuts):
        wait(o_copies[i])
        projected += dot(wv[:, cut].astype(BF16), ov[:, cut], NT)
    rest = stacked(pl.ds(first, h_ref.shape[1] - first), h_ref, h2_ref, hv)
    y_ref[...] = projected
    projected = projected.astype(BF16)
    for i, cut in enumerate(h_cuts):
        wait(h_copies[i])
        store_pieces(pieces, cut, dot(projected, hv[:, cut], NN))
    wait(rest)


def second_term_kernel(y_ref, h_ref, *pieces):
    first = h_ref.shape[1] - pieces[0].shape[1]
    projected = y_ref[...].astype(BF16)
    for cut, units in cuts_of(pieces, first, 2):
        store_pieces(pieces, cut, dot(projected, h_ref[:, units], NN))


def feedback_kernel(w_ref, b_ref, after_ref, first_ref, rest_ref, c_ref):
    q = lax.axis_index("dp") % SQUARE
    rank = w_ref.shape[0]
    rows = rank // SQUARE
    total = jnp.zeros((3 * rank, 3 * rank), F32)
    for cut in chunks(w_ref.shape[1], 4):
        terms = jnp.concatenate(split(w_ref[:, cut], 3), axis=0)
        total += dot(terms, terms, NT)
    total = total[:rank] + total[rank : 2 * rank] + total[2 * rank :]
    c_ref[...] = total[:, :rank] + total[:, rank : 2 * rank] + total[:, 2 * rank :]
    coupling = jnp.concatenate(
        [c_ref[pl.ds((q ^ m) * rows, rows), :] for m in SUMS_AWAY], axis=0
    )
    first = 0
    for ref in (first_ref, rest_ref):
        for cut, units in cuts_of((ref,), first, 2):
            ref[:, cut] = exact_dot(coupling, b_ref[:, units])
        first += ref.shape[1]


def pulled_rows(pieces, f_ref, h_ref, p_ref, first):
    q = lax.axis_index("dp") % SQUARE
    rows = pieces[0].shape[0]
    rank = SQUARE * rows
    pulled = jnp.zeros((2 * rank, h_ref.shape[0]), F32)
    for cut, units in cuts_of(pieces, first, 2):
        p = jnp.concatenate([s[:, cut] for s in pieces], axis=0) - f_ref[:, cut]
        for i, m in enumerate(SUMS_AWAY):
            p_ref[pl.ds((q ^ m) * rows, rows), cut] = p[i * rows : (i + 1) * rows]
        pulled += dot(jnp.concatenate(split(p, 2), axis=0), h_ref[:, units], NT)
    return pulled[:rank] + pulled[rank:]


def gram_terms(p_ref, b_ref, first):
    rank = p_ref.shape[0]
    total = jnp.zeros((3 * rank, 6 * rank), F32)
    for cut, units in cuts_of((p_ref,), first, 2):
        p = split(p_ref[:, cut], 3)
        b = split(b_ref[:, units], 3)
        total += dot(jnp.concatenate(p, axis=0), jnp.concatenate(p + b, axis=0), NT)
    total = total[:rank] + total[rank : 2 * rank] + total[2 * rank :]
    gram = total[:, :rank] + total[:, rank : 2 * rank] + total[:, 2 * rank : 3 * rank]
    cross = total[:, 3 * rank : 4 * rank] + total[:, 4 * rank : 5 * rank] + total[:, 5 * rank :]
    return jnp.concatenate([gram, cross, jnp.zeros((rank, 128 - 2 * rank), F32)], axis=1)


def cuts_of(pieces, first, count):
    cuts = chunks(pieces[0].shape[1], count)
    return [(cut, pl.ds(first + cut.start, cut.size)) for cut in cuts]


def first_pull_kernel(s0, s1, s2, s3, f_ref, h_ref, b_ref, p_ref, v_ref, g_ref):
    v_ref[...] = pulled_rows((s0, s1, s2, s3), f_ref, h_ref, p_ref, 0)
    g_ref[...] = gram_terms(p_ref, b_ref, 0)


def side():
    tensor = lax.axis_index("tensor")
    return (tensor ^ (tensor // 2)) % 2


def pull_kernel(s0, s1, s2, s3, f_ref, h_ref, v_ref, p_ref, keep_ref, send_ref, t_ref):
    q = lax.axis_index("dp") % SQUARE
    mine = side()
    rows, half = s0.shape[0], keep_ref.shape[0]
    first = h_ref.shape[1] - s0.shape[1]
    pulled = v_ref[...] + pulled_rows((s0, s1, s2, s3), f_ref, h_ref, p_ref, first)
    for i, m in enumerate(SUMS_AWAY):
        t_ref[pl.ds((q ^ m) * rows, rows), :] = pulled[i * rows : (i + 1) * rows]
    keep_ref[...] = t_ref[pl.ds(mine * half, half), :]
    send_ref[...] = t_ref[pl.ds((1 - mine) * half, half), :]


def gram_kernel(p_ref, b_ref, g_ref, keep_ref, out_ref):
    grams = g_ref[...] + gram_terms(p_ref, b_ref, b_ref.shape[1] - p_ref.shape[1])
    half, tokens = keep_ref.shape
    out_ref[:, :tokens] = keep_ref[...]
    out_ref[:, tokens : tokens + 128] = grams[:half]
    out_ref[:, tokens + 128 :] = grams[half:]


def push_kernel(mine_ref, got_ref, o_ref, *outs):
    me = lax.axis_index("dp")
    up = lax.axis_index("tensor") // 2
    tokens = o_ref.shape[0]
    half, width = outs[0].shape[1:]
    v = jnp.concatenate(split(mine_ref[:, :tokens] + got_ref[:, :tokens], 2), axis=0)
    for i, m in enumerate(RIGHT_AWAY):
        for z in range(2):
            start = pl.multiple_of((me ^ m ^ (SQUARE * z)) * (2 * width) + up * width, width)
            both = dot(v, o_ref[:, pl.ds(start, width)], NN)
            outs[i][z] = both[:half] + both[half:]


def cholesky_kernel(mine_ref, got_ref, out_ref):
    rank = out_ref.shape[0]
    shape, block = out_ref.shape, 8
    row = lax.broadcasted_iota(jnp.int32, shape, 0)
    lane = lax.broadcasted_iota(jnp.int32, shape, 1)
    grams = mine_ref[...] + got_ref[...]
    grams = jnp.concatenate([grams[:, : shape[1]], grams[:, shape[1] :]], axis=0)
    a = jnp.where(lane == row + 2 * rank, 1.0, grams)
    for k in range(0, rank, block):
        rows = [jnp.broadcast_to(a[k + i : k + i + 1, :], shape) for i in range(block)]
        columns = [jnp.broadcast_to(a[:, k + i : k + i + 1], shape) for i in range(block)]
        change = jnp.zeros(shape, F32)
        for i in range(block):
            inverse = 1.0 / columns[i][k + i : k + i + 1, :]
            change += jnp.where(row > k + i, columns[i], 0.0) * (rows[i] * inverse)
            for j in range(i + 1, block):
                factor = columns[i][k + j : k + j + 1, :] * inverse
                rows[j] = rows[j] - factor * rows[i]
                columns[j] = columns[j] - factor * columns[i]
        a = a - change
    pivots = jnp.sum(jnp.where(lane == row, a, 0.0), axis=1, keepdims=True)
    out_ref[...] = a * (1.0 / jnp.sqrt(pivots))


def near_far_kernel(a_ref, b_ref, c_ref, d_ref, after_ref, near_ref, far_ref):
    near_ref[...] = a_ref[0] + b_ref[0] + c_ref[0] + d_ref[0]
    far_ref[...] = a_ref[1] + b_ref[1] + c_ref[1] + d_ref[1]


def total_kernel(up_far_ref, far_ref, up_near_ref, near_ref, l_ref, after_ref, out_ref, *, replicas):
    up = lax.axis_index("tensor") // 2
    half, width = near_ref.shape
    rank = 2 * half
    inverse = l_ref[:, 2 * rank : 3 * rank] * (1.0 / replicas)
    inverse = jnp.where(side() == 0, inverse[:, :half], inverse[:, half:])
    mine = pl.ds(pl.multiple_of(up * width, width), width)
    other = pl.ds(pl.multiple_of((1 - up) * width, width), width)
    out_ref[:, mine] = exact_dot(inverse, near_ref[...] + far_ref[...])
    out_ref[:, other] = exact_dot(inverse, up_near_ref[...] + up_far_ref[...])


def basis_kernel(p_ref, r_ref, l_ref, w_ref, out_ref, fix_ref, *, norm_scale):
    rank = l_ref.shape[0]
    width = fix_ref.shape[1]
    inverse = l_ref[:, 2 * rank : 3 * rank] * norm_scale
    first = 0
    for ref in (p_ref, r_ref):
        for cut, units in cuts_of((ref,), first, 2):
            out_ref[:, units] = exact_dot(inverse, ref[:, cut])
        first += ref.shape[1]
    own = pl.ds(pl.multiple_of(lax.axis_index("dp") * width, width), width)
    fix_ref[...] = exact_dot(l_ref[:, rank : 2 * rank], w_ref[:, own])


def call(kernel, outs, specs, scratch=(), flops=0, moved=0, vmem=32 << 20):
    return pl.pallas_call(
        kernel,
        out_shape=[jax.ShapeDtypeStruct(shape[:2] if BF16 in shape else shape, BF16 if BF16 in shape else F32) for shape in outs],
        in_specs=specs,
        out_specs=[VMEM_SPEC] * len(outs),
        scratch_shapes=scratch,
        compiler_params=pltpu.CompilerParams(vmem_limit_bytes=vmem),
        cost_estimate=pl.CostEstimate(flops=flops, bytes_accessed=moved, transcendentals=0),
    )


def in_hbm(x):
    return pltpu.with_memory_space_constraint(x, pltpu.HBM)


def swap_dp(x, m):
    n = lax.axis_size("dp")
    return lax.ppermute(x, "dp", [(i, i ^ m) for i in range(n)])


def swap_tensor(x, m):
    n = lax.axis_size("tensor")
    return lax.ppermute(x, "tensor", [(i, i ^ m) for i in range(n)])


def swap_both(x, md, mt):
    n, k = lax.axis_size("dp"), lax.axis_size("tensor")
    pairs = [(i * k + t, (i ^ md) * k + (t ^ mt)) for i in range(n) for t in range(k)]
    return lax.ppermute(x, ("dp", "tensor"), pairs)


def on_device(hidden, out_grad, prev_hidden, prev_grad, prev_basis, warm_start, *, norm_scale):
    replicas = lax.axis_size("dp")
    tokens, units = hidden.shape
    width = out_grad.shape[1]
    rank = warm_start.shape[1]
    rows, half, owned = rank // SQUARE, rank // 2, width // replicas
    w, b = warm_start.T, prev_basis.T
    first = units // 256 * 128
    rest = units - first

    *terms, projected, out_grads, hiddens = call(
        first_term_kernel,
        [(rows, first)] * SQUARE + [(rank, 2 * tokens), (2 * tokens, width, BF16), (2 * tokens, units, BF16)],
        [HBM_SPEC] * 5,
        [pltpu.VMEM((rank, width), F32), pltpu.SemaphoreType.DMA((18,))],
        flops=4 * tokens * rank * (first + width),
        moved=4 * tokens * (units + width) + 4 * rank * (first + width),
    )(*[in_hbm(x) for x in (w, out_grad, prev_grad, hidden, prev_hidden)])
    late_terms = call(
        second_term_kernel,
        [(rows, rest)] * SQUARE,
        [VMEM_SPEC] * 2,
        flops=4 * tokens * rank * rest,
        moved=4 * tokens * rest + 4 * rank * rest,
    )(projected, hiddens)

    def swap_square(x, away):
        return [swap_dp(x[i], m) for i, m in enumerate(away) if m]

    def mean(summed, came):
        own = (summed + came) * (1.0 / replicas)
        return [own] + swap_square([own] * SQUARE, SUMS_AWAY)

    early = terms[0] + sum(swap_square(terms, TERMS_AWAY))
    early_came = swap_dp(early, SQUARE)
    late = late_terms[0] + sum(swap_square(late_terms, TERMS_AWAY))
    late_came = swap_dp(late, SQUARE)
    early_feedback, late_feedback = call(
        feedback_kernel,
        [(rank, first), (rank, rest)],
        [VMEM_SPEC] * 2 + [ANY_SPEC],
        [pltpu.VMEM((rank, rank), F32)],
        flops=2 * rank * rank * (units + width),
        moved=4 * rank * (units + width),
    )(w, b, late)
    early_came, early_feedback = lax.optimization_barrier((early_came, early_feedback))
    early_p = mean(early, early_came)
    late_p = mean(late, late_came)

    p_first, early_v, early_gram = call(
        first_pull_kernel,
        [(rank, first), (rank, 2 * tokens), (rank, 128)],
        [VMEM_SPEC] * 7,
        flops=8 * tokens * rank * first,
        moved=4 * tokens * first + 4 * rank * first,
    )(*early_p, early_feedback, hiddens, b)
    p_rest, keep, send = call(
        pull_kernel,
        [(rank, rest)] + [(half, 2 * tokens)] * 2,
        [VMEM_SPEC] * 7,
        [pltpu.VMEM((rank, 2 * tokens), F32)],
        flops=8 * tokens * rank * rest,
        moved=4 * tokens * rest + 4 * rank * rest,
    )(*late_p, late_feedback, hiddens, early_v)
    other = swap_tensor(send, 1)
    (kept,) = call(
        gram_kernel,
        [(half, 2 * tokens + 256)],
        [VMEM_SPEC] * 4,
        flops=36 * rank * rank * rest,
        moved=8 * rank * rest,
    )(p_rest, b, early_gram, keep)
    plane = kept + jnp.pad(other, ((0, 0), (0, 256)))
    plane_came = swap_both(plane, 0, 3)
    grams = (plane + plane_came)[:, 2 * tokens :]
    grams_came = swap_tensor(grams, 1)
    parts = call(
        push_kernel,
        [(2, half, owned // 2)] * SQUARE,
        [VMEM_SPEC] * 3,
        flops=8 * tokens * half * width,
        moved=4 * tokens * width + 4 * half * width,
    )(plane, plane_came, out_grads)
    came = swap_square(parts, RIGHT_AWAY)
    (solved,) = call(
        cholesky_kernel, [(rank, 128)], [VMEM_SPEC] * 2, flops=rank**3, moved=8 * rank * 128
    )(grams, grams_came)
    near, far = call(
        near_far_kernel,
        [(half, owned // 2)] * 2,
        [VMEM_SPEC] * 4 + [ANY_SPEC],
        flops=6 * half * owned,
        moved=40 * half * owned,
    )(parts[0], *came, solved)
    basis, fix = call(
        functools.partial(basis_kernel, norm_scale=norm_scale),
        [(rank, units), (rank, owned)],
        [VMEM_SPEC] * 4,
        flops=2 * rank * rank * units,
        moved=8 * rank * units,
    )(p_first, p_rest, solved, w)
    up_far = swap_both(far, SQUARE, 3)
    far_came = swap_both(far, SQUARE, 0)
    up_near = swap_both(near, 0, 3)
    (mine,) = call(
        functools.partial(total_kernel, replicas=replicas),
        [(rank, owned)],
        [VMEM_SPEC] * 5 + [ANY_SPEC],
        flops=rank * rank * owned,
        moved=12 * half * owned,
    )(up_far, far_came, up_near, near, solved, fix)
    factor = mine + swap_tensor(mine, 1) - fix
    return (basis.T, factor.T)


def fits(mesh, dp=8, tensor=4):
    return mesh.shape["dp"] == dp and mesh.shape["tensor"] == tensor


def solution(mesh):
    def whole(hidden, out_grad, prev_hidden, prev_grad, prev_basis, warm_start):
        norm_scale = float(prev_basis.shape[0]) ** 0.5
        body = on_device if fits(mesh) else plain_on_device
        return jax.shard_map(
            functools.partial(body, norm_scale=norm_scale),
            mesh=mesh,
            in_specs=(
                P("dp", "tensor"),
                P("dp", None),
                P("dp", "tensor"),
                P("dp", None),
                P("tensor", None),
                P(),
            ),
            out_specs=(P("tensor", None), P("dp", None)),
            check_vma=False,
        )(hidden, out_grad, prev_hidden, prev_grad, prev_basis, warm_start)

    return whole
```

```python
import functools

import jax
import jax.numpy as jnp
from jax import lax
from jax.experimental import pallas as pl
from jax.experimental.pallas import tpu as pltpu
from jax.sharding import PartitionSpec as P

F32 = jnp.float32
BF16 = jnp.bfloat16
SQUARE = 4
TERMS_AWAY = (0, 3, 2, 1)
SUMS_AWAY = (0, 3, 2, 1)
RIGHT_AWAY = (0, 3, 2, 1)
NT = (((1,), (1,)), ((), ()))
NN = (((1,), (0,)), ((), ()))
VMEM_SPEC = pl.BlockSpec(memory_space=pltpu.VMEM)
ANY_SPEC = pl.BlockSpec(memory_space=pl.ANY)
HBM_SPEC = pl.BlockSpec(memory_space=pltpu.HBM)


def orthonormal(rows_in, gram_matrix, norm_scale):
    lower = jnp.linalg.cholesky(gram_matrix)
    return norm_scale * jax.scipy.linalg.solve_triangular(lower, rows_in.T, lower=True).T


def plain_on_device(hidden, out_grad, prev_hidden, prev_grad, prev_basis, warm_start, *, norm_scale):
    highest = lax.Precision.HIGHEST
    replicas = lax.axis_size("dp")
    warm_low = warm_start.astype(BF16)
    projected = jnp.dot(out_grad, warm_low, preferred_element_type=F32).astype(BF16)
    projected_prev = jnp.dot(prev_grad, warm_low, preferred_element_type=F32).astype(BF16)
    coupling = jnp.dot(warm_start.T, warm_start, precision=highest)
    summed = jnp.einsum("tf,tr->fr", hidden, projected, preferred_element_type=F32)
    summed = summed + jnp.einsum(
        "tf,tr->fr", prev_hidden, projected_prev, preferred_element_type=F32
    )
    local_p = (summed - jnp.dot(prev_basis, coupling, precision=highest)) / replicas
    p_mean = lax.psum(local_p, "dp")
    gram_matrix = lax.psum(jnp.dot(p_mean.T, p_mean, precision=highest), "tensor")
    new_basis = orthonormal(p_mean, gram_matrix, norm_scale)
    basis_low = new_basis.astype(BF16)
    pulled = jnp.dot(hidden, basis_low, preferred_element_type=F32).astype(BF16)
    pulled_prev = jnp.dot(prev_hidden, basis_low, preferred_element_type=F32).astype(BF16)
    cross_basis = jnp.dot(prev_basis.T, new_basis, precision=highest)
    summed_q = jnp.einsum("td,tr->dr", out_grad, pulled, preferred_element_type=F32)
    summed_q = summed_q + jnp.einsum(
        "td,tr->dr", prev_grad, pulled_prev, preferred_element_type=F32
    )
    local_q = (summed_q - jnp.dot(warm_start, cross_basis, precision=highest)) / replicas
    row_count = warm_start.shape[0] // replicas
    summed_all = lax.psum(local_q, ("dp", "tensor"))
    owned_rows = lax.dynamic_slice_in_dim(
        summed_all, lax.axis_index("dp") * row_count, row_count, 0
    )
    return (new_basis, owned_rows / norm_scale)


def split(x, terms):
    parts = []
    for i in range(terms):
        part = x.astype(BF16)
        parts.append(part)
        if i + 1 < terms:
            x = x - part.astype(F32)
    return parts


def dot(a, b, dims, precision=None):
    return lax.dot_general(a, b, dims, preferred_element_type=F32, precision=precision)


def exact_dot(a, b):
    a1, a2, a3 = split(a, 3)
    b1, b2, b3 = split(b, 3)
    left = jnp.concatenate([a1, a1, a1, a2, a2, a3], axis=1)
    right = jnp.concatenate([b1, b2, b3, b1, b2, b1], axis=0)
    return dot(left, right, NN)


def chunks(extent, count):
    step = extent // count
    return [pl.ds(i * step, step) for i in range(count)]


def store_pieces(pieces, cut, summed):
    rows = pieces[0].shape[0]
    for i, piece in enumerate(pieces):
        piece[:, cut] = summed[i * rows : (i + 1) * rows]


def first_term_kernel(w_ref, o_ref, o2_ref, h_ref, h2_ref, *refs):
    pieces, (y_ref, ov, hv, wv, sem) = refs[:SQUARE], refs[SQUARE:]
    q = lax.axis_index("dp") % SQUARE
    rows = wv.shape[0] // SQUARE
    tokens = o_ref.shape[0]
    first = pieces[0].shape[1]
    copies = []

    def copy(source, target):
        copies.append(pltpu.make_async_copy(source, target, sem.at[len(copies)]))
        copies[-1].start()
        return copies[-1]

    def stacked(cut, ref, ref2, target):
        return [
            copy(r.at[:, cut], target.at[pl.ds(j * tokens, tokens), cut]) for j, r in enumerate((ref, ref2))
        ]

    def wait(pending):
        for c in pending:
            c.wait()

    o_cuts, h_cuts = chunks(o_ref.shape[1], 4), chunks(first, 2)
    w_copies = [
        copy(w_ref.at[pl.ds((q ^ m) * rows, rows), :], wv.at[pl.ds(i * rows, rows), :])
        for i, m in enumerate(TERMS_AWAY)
    ]
    o_copies = [stacked(cut, o_ref, o2_ref, ov) for cut in o_cuts]
    h_copies = [stacked(cut, h_ref, h2_ref, hv) for cut in h_cuts]
    wait(w_copies)
    projected = jnp.zeros((wv.shape[0], 2 * tokens), F32)
    for i, cut in enumerate(o_cuts):
        wait(o_copies[i])
        projected += dot(wv[:, cut].astype(BF16), ov[:, cut], NT)
    rest = stacked(pl.ds(first, h_ref.shape[1] - first), h_ref, h2_ref, hv)
    y_ref[...] = projected
    projected = projected.astype(BF16)
    for i, cut in enumerate(h_cuts):
        wait(h_copies[i])
        store_pieces(pieces, cut, dot(projected, hv[:, cut], NN))
    wait(rest)


def second_term_kernel(y_ref, h_ref, *pieces):
    first = h_ref.shape[1] - pieces[0].shape[1]
    projected = y_ref[...].astype(BF16)
    for cut, units in cuts_of(pieces, first, 2):
        store_pieces(pieces, cut, dot(projected, h_ref[:, units], NN))


def feedback_kernel(w_ref, b_ref, after_ref, first_ref, rest_ref, c_ref):
    q = lax.axis_index("dp") % SQUARE
    rank = w_ref.shape[0]
    rows = rank // SQUARE
    total = jnp.zeros((3 * rank, 3 * rank), F32)
    for cut in chunks(w_ref.shape[1], 4):
        terms = jnp.concatenate(split(w_ref[:, cut], 3), axis=0)
        total += dot(terms, terms, NT)
    total = total[:rank] + total[rank : 2 * rank] + total[2 * rank :]
    c_ref[...] = total[:, :rank] + total[:, rank : 2 * rank] + total[:, 2 * rank :]
    coupling = jnp.concatenate(
        [c_ref[pl.ds((q ^ m) * rows, rows), :] for m in SUMS_AWAY], axis=0
    )
    first = 0
    for ref in (first_ref, rest_ref):
        for cut, units in cuts_of((ref,), first, 2):
            ref[:, cut] = exact_dot(coupling, b_ref[:, units])
        first += ref.shape[1]


def pulled_rows(pieces, f_ref, h_ref, p_ref, first):
    q = lax.axis_index("dp") % SQUARE
    rows = pieces[0].shape[0]
    rank = SQUARE * rows
    pulled = jnp.zeros((2 * rank, h_ref.shape[0]), F32)
    for cut, units in cuts_of(pieces, first, 2):
        p = jnp.concatenate([s[:, cut] for s in pieces], axis=0) - f_ref[:, cut]
        for i, m in enumerate(SUMS_AWAY):
            p_ref[pl.ds((q ^ m) * rows, rows), cut] = p[i * rows : (i + 1) * rows]
        pulled += dot(jnp.concatenate(split(p, 2), axis=0), h_ref[:, units], NT)
    return pulled[:rank] + pulled[rank:]


def gram_terms(p_ref, b_ref, first):
    rank = p_ref.shape[0]
    total = jnp.zeros((3 * rank, 6 * rank), F32)
    for cut, units in cuts_of((p_ref,), first, 2):
        p = split(p_ref[:, cut], 3)
        b = split(b_ref[:, units], 3)
        total += dot(jnp.concatenate(p, axis=0), jnp.concatenate(p + b, axis=0), NT)
    total = total[:rank] + total[rank : 2 * rank] + total[2 * rank :]
    gram = total[:, :rank] + total[:, rank : 2 * rank] + total[:, 2 * rank : 3 * rank]
    cross = total[:, 3 * rank : 4 * rank] + total[:, 4 * rank : 5 * rank] + total[:, 5 * rank :]
    return jnp.concatenate([gram, cross, jnp.zeros((rank, 128 - 2 * rank), F32)], axis=1)


def cuts_of(pieces, first, count):
    cuts = chunks(pieces[0].shape[1], count)
    return [(cut, pl.ds(first + cut.start, cut.size)) for cut in cuts]


def first_pull_kernel(s0, s1, s2, s3, f_ref, h_ref, b_ref, p_ref, v_ref, g_ref):
    v_ref[...] = pulled_rows((s0, s1, s2, s3), f_ref, h_ref, p_ref, 0)
    g_ref[...] = gram_terms(p_ref, b_ref, 0)


def side():
    tensor = lax.axis_index("tensor")
    return (tensor ^ (tensor // 2)) % 2


def pull_kernel(s0, s1, s2, s3, f_ref, h_ref, v_ref, p_ref, keep_ref, send_ref, t_ref):
    q = lax.axis_index("dp") % SQUARE
    mine = side()
    rows, half = s0.shape[0], keep_ref.shape[0]
    first = h_ref.shape[1] - s0.shape[1]
    pulled = v_ref[...] + pulled_rows((s0, s1, s2, s3), f_ref, h_ref, p_ref, first)
    for i, m in enumerate(SUMS_AWAY):
        t_ref[pl.ds((q ^ m) * rows, rows), :] = pulled[i * rows : (i + 1) * rows]
    keep_ref[...] = t_ref[pl.ds(mine * half, half), :]
    send_ref[...] = t_ref[pl.ds((1 - mine) * half, half), :]


def gram_kernel(p_ref, b_ref, g_ref, keep_ref, out_ref):
    grams = g_ref[...] + gram_terms(p_ref, b_ref, b_ref.shape[1] - p_ref.shape[1])
    half, tokens = keep_ref.shape
    out_ref[:, :tokens] = keep_ref[...]
    out_ref[:, tokens : tokens + 128] = grams[:half]
    out_ref[:, tokens + 128 :] = grams[half:]


def push_kernel(mine_ref, got_ref, o_ref, *outs):
    me = lax.axis_index("dp")
    up = lax.axis_index("tensor") // 2
    tokens = o_ref.shape[0]
    half, width = outs[0].shape[1:]
    v = jnp.concatenate(split(mine_ref[:, :tokens] + got_ref[:, :tokens], 2), axis=0)
    for i, m in enumerate(RIGHT_AWAY):
        for z in range(2):
            start = pl.multiple_of((me ^ m ^ (SQUARE * z)) * (2 * width) + up * width, width)
            both = dot(v, o_ref[:, pl.ds(start, width)], NN)
            outs[i][z] = both[:half] + both[half:]


def cholesky_kernel(mine_ref, got_ref, out_ref):
    rank = out_ref.shape[0]
    shape, block = out_ref.shape, 8
    row = lax.broadcasted_iota(jnp.int32, shape, 0)
    lane = lax.broadcasted_iota(jnp.int32, shape, 1)
    grams = mine_ref[...] + got_ref[...]
    grams = jnp.concatenate([grams[:, : shape[1]], grams[:, shape[1] :]], axis=0)
    a = jnp.where(lane == row + 2 * rank, 1.0, grams)
    for k in range(0, rank, block):
        rows = [jnp.broadcast_to(a[k + i : k + i + 1, :], shape) for i in range(block)]
        columns = [jnp.broadcast_to(a[:, k + i : k + i + 1], shape) for i in range(block)]
        change = jnp.zeros(shape, F32)
        for i in range(block):
            inverse = 1.0 / columns[i][k + i : k + i + 1, :]
            change += jnp.where(row > k + i, columns[i], 0.0) * (rows[i] * inverse)
            for j in range(i + 1, block):
                factor = columns[i][k + j : k + j + 1, :] * inverse
                rows[j] = rows[j] - factor * rows[i]
                columns[j] = columns[j] - factor * columns[i]
        a = a - change
    pivots = jnp.sum(jnp.where(lane == row, a, 0.0), axis=1, keepdims=True)
    out_ref[...] = a * (1.0 / jnp.sqrt(pivots))


def near_far_kernel(a_ref, b_ref, c_ref, d_ref, after_ref, near_ref, far_ref):
    near_ref[...] = a_ref[0] + b_ref[0] + c_ref[0] + d_ref[0]
    far_ref[...] = a_ref[1] + b_ref[1] + c_ref[1] + d_ref[1]


def total_kernel(up_far_ref, far_ref, up_near_ref, near_ref, after_ref, out_ref):
    up = lax.axis_index("tensor") // 2
    width = near_ref.shape[1]
    mine = pl.ds(pl.multiple_of(up * width, width), width)
    other = pl.ds(pl.multiple_of((1 - up) * width, width), width)
    out_ref[:, mine] = near_ref[...] + far_ref[...]
    out_ref[:, other] = up_near_ref[...] + up_far_ref[...]


def basis_kernel(p_ref, r_ref, l_ref, w_ref, out_ref, fix_ref, *, norm_scale):
    rank = l_ref.shape[0]
    width = fix_ref.shape[1]
    inverse = l_ref[:, 2 * rank : 3 * rank] * norm_scale
    first = 0
    for ref in (p_ref, r_ref):
        for cut, units in cuts_of((ref,), first, 2):
            out_ref[:, units] = exact_dot(inverse, ref[:, cut])
        first += ref.shape[1]
    own = pl.ds(pl.multiple_of(lax.axis_index("dp") * width, width), width)
    fix_ref[...] = exact_dot(l_ref[:, rank : 2 * rank], w_ref[:, own])


def factor_kernel(t_ref, u_ref, l_ref, fix_ref, out_ref, z_ref, *, replicas):
    mine = side()
    half = t_ref.shape[0]
    rank = 2 * half
    z_ref[pl.ds(mine * half, half), :] = t_ref[...]
    z_ref[pl.ds((1 - mine) * half, half), :] = u_ref[...]
    inverse = l_ref[:, 2 * rank : 3 * rank] * (1.0 / replicas)
    out_ref[...] = exact_dot(inverse, z_ref[...]) - fix_ref[...]


def call(kernel, outs, specs, scratch=(), flops=0, moved=0, vmem=32 << 20):
    return pl.pallas_call(
        kernel,
        out_shape=[jax.ShapeDtypeStruct(shape[:2] if BF16 in shape else shape, BF16 if BF16 in shape else F32) for shape in outs],
        in_specs=specs,
        out_specs=[VMEM_SPEC] * len(outs),
        scratch_shapes=scratch,
        compiler_params=pltpu.CompilerParams(vmem_limit_bytes=vmem),
        cost_estimate=pl.CostEstimate(flops=flops, bytes_accessed=moved, transcendentals=0),
    )


def in_hbm(x):
    return pltpu.with_memory_space_constraint(x, pltpu.HBM)


def swap_dp(x, m):
    n = lax.axis_size("dp")
    return lax.ppermute(x, "dp", [(i, i ^ m) for i in range(n)])


def swap_tensor(x, m):
    n = lax.axis_size("tensor")
    return lax.ppermute(x, "tensor", [(i, i ^ m) for i in range(n)])


def swap_both(x, md, mt):
    n, k = lax.axis_size("dp"), lax.axis_size("tensor")
    pairs = [(i * k + t, (i ^ md) * k + (t ^ mt)) for i in range(n) for t in range(k)]
    return lax.ppermute(x, ("dp", "tensor"), pairs)


def on_device(hidden, out_grad, prev_hidden, prev_grad, prev_basis, warm_start, *, norm_scale):
    replicas = lax.axis_size("dp")
    tokens, units = hidden.shape
    width = out_grad.shape[1]
    rank = warm_start.shape[1]
    rows, half, owned = rank // SQUARE, rank // 2, width // replicas
    w, b = warm_start.T, prev_basis.T
    first = units // 256 * 128
    rest = units - first

    *terms, projected, out_grads, hiddens = call(
        first_term_kernel,
        [(rows, first)] * SQUARE + [(rank, 2 * tokens), (2 * tokens, width, BF16), (2 * tokens, units, BF16)],
        [HBM_SPEC] * 5,
        [pltpu.VMEM((rank, width), F32), pltpu.SemaphoreType.DMA((18,))],
        flops=4 * tokens * rank * (first + width),
        moved=4 * tokens * (units + width) + 4 * rank * (first + width),
    )(*[in_hbm(x) for x in (w, out_grad, prev_grad, hidden, prev_hidden)])
    late_terms = call(
        second_term_kernel,
        [(rows, rest)] * SQUARE,
        [VMEM_SPEC] * 2,
        flops=4 * tokens * rank * rest,
        moved=4 * tokens * rest + 4 * rank * rest,
    )(projected, hiddens)

    def swap_square(x, away):
        return [swap_dp(x[i], m) for i, m in enumerate(away) if m]

    def mean(summed, came):
        own = (summed + came) * (1.0 / replicas)
        return [own] + swap_square([own] * SQUARE, SUMS_AWAY)

    got = swap_square(terms, TERMS_AWAY)
    got[1], late_terms = lax.optimization_barrier((got[1], late_terms))
    early = terms[0] + sum(got)
    early_came = swap_dp(early, SQUARE)
    late = late_terms[0] + sum(swap_square(late_terms, TERMS_AWAY))
    late_came = swap_dp(late, SQUARE)
    early_feedback, late_feedback = call(
        feedback_kernel,
        [(rank, first), (rank, rest)],
        [VMEM_SPEC] * 2 + [ANY_SPEC],
        [pltpu.VMEM((rank, rank), F32)],
        flops=2 * rank * rank * (units + width),
        moved=4 * rank * (units + width),
    )(w, b, late)
    early_came, early_feedback = lax.optimization_barrier((early_came, early_feedback))
    early_p = mean(early, early_came)
    late_p = mean(late, late_came)

    p_first, early_v, early_gram = call(
        first_pull_kernel,
        [(rank, first), (rank, 2 * tokens), (rank, 128)],
        [VMEM_SPEC] * 7,
        flops=8 * tokens * rank * first,
        moved=4 * tokens * first + 4 * rank * first,
    )(*early_p, early_feedback, hiddens, b)
    p_rest, keep, send = call(
        pull_kernel,
        [(rank, rest)] + [(half, 2 * tokens)] * 2,
        [VMEM_SPEC] * 7,
        [pltpu.VMEM((rank, 2 * tokens), F32)],
        flops=8 * tokens * rank * rest,
        moved=4 * tokens * rest + 4 * rank * rest,
    )(*late_p, late_feedback, hiddens, early_v)
    other = swap_tensor(send, 1)
    (kept,) = call(
        gram_kernel,
        [(half, 2 * tokens + 256)],
        [VMEM_SPEC] * 4,
        flops=36 * rank * rank * rest,
        moved=8 * rank * rest,
    )(p_rest, b, early_gram, keep)
    plane = kept + jnp.pad(other, ((0, 0), (0, 256)))
    plane_came = swap_both(plane, 0, 3)
    grams = (plane + plane_came)[:, 2 * tokens :]
    grams_came = swap_tensor(grams, 1)
    parts = call(
        push_kernel,
        [(2, half, owned // 2)] * SQUARE,
        [VMEM_SPEC] * 3,
        flops=8 * tokens * half * width,
        moved=4 * tokens * width + 4 * half * width,
    )(plane, plane_came, out_grads)
    came = swap_square(parts, RIGHT_AWAY)
    (solved,) = call(
        cholesky_kernel, [(rank, 128)], [VMEM_SPEC] * 2, flops=rank**3, moved=8 * rank * 128
    )(grams, grams_came)
    near, far = call(
        near_far_kernel,
        [(half, owned // 2)] * 2,
        [VMEM_SPEC] * 4 + [ANY_SPEC],
        flops=6 * half * owned,
        moved=40 * half * owned,
    )(parts[0], *came, solved)
    basis, fix = call(
        functools.partial(basis_kernel, norm_scale=norm_scale),
        [(rank, units), (rank, owned)],
        [VMEM_SPEC] * 4,
        flops=2 * rank * rank * units,
        moved=8 * rank * units,
    )(p_first, p_rest, solved, w)
    up_far = swap_both(far, SQUARE, 3)
    far_came = swap_both(far, SQUARE, 0)
    up_near = swap_both(near, 0, 3)
    (mine,) = call(
        total_kernel,
        [(half, owned)],
        [VMEM_SPEC] * 4 + [ANY_SPEC],
        flops=half * owned,
        moved=12 * half * owned,
    )(up_far, far_came, up_near, near, fix)
    (factor,) = call(
        functools.partial(factor_kernel, replicas=replicas),
        [(rank, owned)],
        [VMEM_SPEC] * 4,
        [pltpu.VMEM((rank, owned), F32)],
        flops=2 * rank * rank * owned,
        moved=12 * rank * owned,
    )(mine, swap_tensor(mine, 1), solved, fix)
    return (basis.T, factor.T)


def fits(mesh, dp=8, tensor=4):
    return mesh.shape["dp"] == dp and mesh.shape["tensor"] == tensor


def solution(mesh):
    def whole(hidden, out_grad, prev_hidden, prev_grad, prev_basis, warm_start):
        norm_scale = float(prev_basis.shape[0]) ** 0.5
        body = on_device if fits(mesh) else plain_on_device
        return jax.shard_map(
            functools.partial(body, norm_scale=norm_scale),
            mesh=mesh,
            in_specs=(
                P("dp", "tensor"),
                P("dp", None),
                P("dp", "tensor"),
                P("dp", None),
                P("tensor", None),
                P(),
            ),
            out_specs=(P("tensor", None), P("dp", None)),
            check_vma=False,
        )(hidden, out_grad, prev_hidden, prev_grad, prev_basis, warm_start)

    return whole
```
